768 devices in a mesh: src: 12 (over z), freq: 2 (over y_hi), space: 32 (over x, y_lo, core).
Axes of the slice: x: 4, y: 8 (y_hi: 2, y_lo: 4; y = y_hi * 4 + y_lo), z: 12, core: 2. Of those that a mesh axis runs over, the one named last changes fastest.
Arguments:
- forward_field: float32 [12, 16, 2, 64, 3072], P('src', 'freq', None, 'space'), may hold values from -6 to 6
- adjoint_field: float32 [12, 16, 2, 64, 3072], P('src', 'freq', None, 'space'), may hold values from -6 to 6
- source_group: int32 [12], P('src'), may hold values from 0 to 2, as said below
- group_weight: float32 [3], replicated, may hold values from 0.5 to 2
- frequency_index: int32 [16], replicated, may hold values from 0 to 15, each once
- log_sigma: float32 [64, 3072], P('space', ('src', 'freq')), may hold values from -1 to 1
- charge: float32 [64, 3072], P('space', ('src', 'freq')), may hold values from 0.05 to 0.6
- log_tau: float32 [64, 3072], P('space', ('src', 'freq')), may hold values from -6.9 to 0
- exponent: float32 [64, 3072], P('space', ('src', 'freq')), may hold values from 0.2 to 0.8
- active: int32 [64, 3072], P('space', ('src', 'freq')), may hold values 0 or 1
- prior_weight: float32 [4, 3], replicated, may hold values from 0.03 to 0.15
Outputs:
- smoothed: float32 [4, 64, 3072], P(None, 'space', ('src', 'freq'))
The draws below stay inside these ranges and needn't reach their ends.
Inputs may be any that keep to these rules, and one draw needn't show every extreme that they name: `source_group`: every one of the 3 groups holds at least one source. `frequency_index`: A permutation of the frequency list positions.
All inputs are finite; a program needn't handle non-finite values. No bound on the sum of `active` on one device may be relied on, other than what follows from the above.
Results may differ from the reference program's by a relative error of at most 0.0002.
Values sent between devices are 32-bit elements; how exact they have to be, the bound alone decides.
A program may use at most 64 MiB of HBM per device.

```python
import math
import jax
import jax.numpy as jnp
from jax import lax

FREQ = 16
GROUPS = 3
NY = 64
SOURCES = 12
NX = 64
NZ = 48


def draw_source_group(key, part):
    order = jax.random.permutation(key, SOURCES)
    return (order % GROUPS).astype(jnp.int32)


def set_ends(values, stream_key, low, high):
    place = [jax.random.randint(jax.random.fold_in(stream_key, axis), (), 0, length) for axis, length in enumerate(values.shape)]
    widest = values.shape.index(max(values.shape))
    next_to = place[:widest] + [(place[widest] + 1) % values.shape[widest]] + place[widest + 1:]
    return values.at[tuple(place)].set(low).at[tuple(next_to)].set(high)


def level_of(rng, extent, shards, smallest, top_value):
    loudness = 1.0
    for position, parts in shards:
        heights = jax.random.uniform(jax.random.fold_in(jax.random.fold_in(rng, 6), position), (parts,), jnp.float32, smallest / len(shards), top_value / len(shards))
        loudness = loudness * jnp.repeat(jnp.exp(heights), extent[position] // parts).reshape((-1,) + (1,) * (len(extent) - 1 - position))
    return loudness


def bell_draw(rng, shape, spread, limit, pieces=(), kind=jnp.bfloat16):
    values = jax.random.normal(rng, shape, jnp.float32) * spread
    if len(pieces) > 0:
        values = level_of(rng, shape, pieces, -0.22, 0.18) * values
    return jnp.clip(values, min=-limit, max=limit).astype(kind)


def setup_inputs(seed: int = 0) -> dict:
    key_of = jax.random.split(jax.random.key(seed), 12)
    forward_field = bell_draw(key_of[0], (SOURCES, FREQ, 2, NX, NZ * NY), 1.0, 6.0, ((0, 12), (1, 2), (3, 32)), jnp.float32)
    adjoint_field = bell_draw(key_of[1], (SOURCES, FREQ, 2, NX, NZ * NY), 1.0, 6.0, ((0, 12), (1, 2), (3, 32)), jnp.float32)
    source_group = draw_source_group(jax.random.fold_in(key_of[11], 71), 0)
    group_weight = jnp.clip(jnp.exp(jax.random.uniform(key_of[3], (GROUPS,), jnp.float32, math.log(0.5), math.log(2.0))), 0.5, 2.0)
    frequency_index = jax.random.permutation(key_of[4], FREQ).astype(jnp.int32)
    log_sigma = jnp.clip(jax.random.uniform(key_of[5], (NX, NZ * NY), jnp.float32, -1.0, 1.0) * level_of(key_of[5], (NX, NZ * NY), ((0, 32), (1, 24)), -0.4, 0.0), -1.0, 1.0)
    charge = jnp.clip(0.05 + 0.55 * jax.random.uniform(key_of[6], (NX, NZ * NY), jnp.float32) ** level_of(key_of[6], (NX, NZ * NY), ((0, 32), (1, 24)), -0.2, 0.2), 0.05, 0.6)
    log_tau = jnp.clip(-6.9 + 6.9 * jax.random.uniform(key_of[7], (NX, NZ * NY), jnp.float32) ** level_of(key_of[7], (NX, NZ * NY), ((0, 32), (1, 24)), -0.2, 0.2), -6.9, 0.0)
    exponent = jnp.clip(0.2 + 0.6 * jax.random.uniform(key_of[8], (NX, NZ * NY), jnp.float32) ** level_of(key_of[8], (NX, NZ * NY), ((0, 32), (1, 24)), -0.2, 0.2), 0.2, 0.8)
    active = set_ends((jax.random.randint(key_of[9], (NX, NZ * NY), 0, 4) < 3).astype(jnp.int32), jax.random.fold_in(key_of[9], 1), 0, 1)
    prior_weight = jnp.clip(jnp.exp(jax.random.uniform(key_of[10], (4, 3), jnp.float32, math.log(0.03), math.log(0.15))), 0.03, 0.15)
    return {"forward_field": forward_field, "adjoint_field": adjoint_field, "source_group": source_group, "group_weight": group_weight, "frequency_index": frequency_index, "log_sigma": log_sigma, "charge": charge, "log_tau": log_tau, "exponent": exponent, "active": active, "prior_weight": prior_weight}


def gradients(extended, y_cells):
    grad_x = 0.5 * (extended[..., 2:, :] - extended[..., :-2, :])
    centre = extended[..., 1:-1, :]
    cells = centre.shape[-1]
    z_padding = [(0, 0)] * (centre.ndim - 1) + [(y_cells, y_cells)]
    padded = jnp.pad(centre, z_padding)
    grad_z = 0.5 * (padded[..., 2 * y_cells:] - padded[..., :cells])
    y_padding = [(0, 0)] * (centre.ndim - 1) + [(1, 1)]
    padded = jnp.pad(centre, y_padding)
    y_pos = jnp.arange(cells, dtype=jnp.int32) % y_cells
    upper = jnp.where(y_pos < y_cells - 1, padded[..., 2:], 0.0)
    lower = jnp.where(y_pos > 0, padded[..., :-2], 0.0)
    grad_y = 0.5 * (upper - lower)
    return (grad_x, grad_y, grad_z)

def correlate(grad_parts):
    real_sum = 0.0
    imag_sum = 0.0
    for grad_part in grad_parts:
        forward_real = grad_part[0][:, :, 0]
        forward_imag = grad_part[0][:, :, 1]
        adjoint_real = grad_part[1][:, :, 0]
        adjoint_imag = grad_part[1][:, :, 1]
        real_sum = real_sum + forward_real * adjoint_real - forward_imag * adjoint_imag
        imag_sum = imag_sum + forward_real * adjoint_imag + forward_imag * adjoint_real
    return jnp.stack([real_sum, imag_sum], axis=2)

def freq_omega(index_list, count):
    return 2.0 * math.pi * jnp.exp(math.log(10.0) * (-1.0 + 4.0 * index_list.astype(jnp.float32) / (count - 1)))

def complex_product(left_real, left_imag, right_real, right_imag):
    return (left_real * right_real - left_imag * right_imag, left_real * right_imag + left_imag * right_real)

def chain_rule(correlation, omega_list, log_sigma, charge, log_tau, exponent, scale_factor):
    omega_list = omega_list.reshape(omega_list.shape + (1,) * log_sigma.ndim)
    log_product = jnp.log(omega_list) + log_tau
    amplitude = jnp.exp(exponent * log_product)
    phase_angle = exponent * (0.5 * math.pi)
    zeta_real = amplitude * jnp.cos(phase_angle)
    zeta_imag = amplitude * jnp.sin(phase_angle)
    sigma_zero = jnp.exp(log_sigma)
    denom_real = 1.0 + (1.0 - charge) * zeta_real
    denom_imag = (1.0 - charge) * zeta_imag
    inverse = 1.0 / (denom_real * denom_real + denom_imag * denom_imag)
    recip_real = denom_real * inverse
    recip_imag = -denom_imag * inverse
    sigma_real, sigma_imag = complex_product(1.0 + zeta_real, zeta_imag, recip_real, recip_imag)
    square_real, square_imag = complex_product(recip_real, recip_imag, recip_real, recip_imag)
    numer_real, numer_imag = complex_product(1.0 + zeta_real, zeta_imag, zeta_real, zeta_imag)
    charge_real, charge_imag = complex_product(numer_real, numer_imag, square_real, square_imag)
    slope_real, slope_imag = complex_product(charge * square_real, charge * square_imag, zeta_real, zeta_imag)
    expo_real, expo_imag = complex_product(slope_real, slope_imag, log_product, 0.5 * math.pi)
    derivs = ((sigma_real, sigma_imag), (charge_real, charge_imag), (exponent * slope_real, exponent * slope_imag), (expo_real, expo_imag))
    corr_real = correlation[:, 0]
    corr_imag = correlation[:, 1]
    rows_out = []
    for part_real, part_imag in derivs:
        rows_out.append(sigma_zero * lax.optimization_barrier(jnp.sum(part_real * corr_real - part_imag * corr_imag, axis=0)))
    return jnp.stack(rows_out) * scale_factor

def smooth_pass(extended, prior_weight):
    centre = extended[:, 1:-1, 1:-1, :]
    along_x = extended[:, 2:, 1:-1, :] + extended[:, :-2, 1:-1, :] - 2.0 * centre
    along_z = extended[:, 1:-1, 2:, :] + extended[:, 1:-1, :-2, :] - 2.0 * centre
    padded = jnp.pad(centre, ((0, 0), (0, 0), (0, 0), (1, 1)))
    along_y = padded[..., 2:] + padded[..., :-2] - 2.0 * centre
    weight_x = prior_weight[:, 0].reshape(-1, 1, 1, 1)
    weight_y = prior_weight[:, 1].reshape(-1, 1, 1, 1)
    weight_z = prior_weight[:, 2].reshape(-1, 1, 1, 1)
    return centre + weight_x * along_x + weight_y * along_y + weight_z * along_z

def reference(forward_field, adjoint_field, source_group, group_weight, frequency_index, log_sigma, charge, log_tau, exponent, active, prior_weight):
    source_weight = lax.optimization_barrier(jnp.sum(jnp.where(source_group[:, None] == jnp.arange(GROUPS)[None, :], group_weight[None, :], 0.0), axis=1))

    def accumulate(running, sliced):
        forward_one, adjoint_one, weight_one = sliced
        stacked = jnp.stack([forward_one, adjoint_one])[:, None]
        extended = jnp.pad(stacked, ((0, 0), (0, 0), (0, 0), (0, 0), (1, 1), (0, 0)))
        correlation = correlate(gradients(extended, NY))[0]
        return (running + weight_one * correlation, None)
    start_value = jnp.zeros((FREQ, 2, NX, NZ * NY), forward_field.dtype)
    total, _ = lax.scan(accumulate, start_value, (forward_field, adjoint_field, source_weight))
    correlation = total.reshape(FREQ, 2, NX, NZ * NY)
    omega_list = freq_omega(frequency_index, FREQ)
    scale_factor = 1.0 / math.sqrt(SOURCES * FREQ)
    gradient = chain_rule(correlation, omega_list, log_sigma, charge, log_tau, exponent, scale_factor)
    masked = gradient * active.astype(jnp.float32)
    smooth_field = masked.reshape(4, NX, NZ, NY)
    for step_index in range(2):
        extended = jnp.pad(smooth_field, ((0, 0), (1, 1), (1, 1), (0, 0)))
        smooth_field = smooth_pass(extended, prior_weight)
    return smooth_field.reshape(4, NX, NZ * NY)
```

```python
import functools
import math

import jax
import jax.numpy as jnp
from jax import lax
from jax.experimental import pallas as pl
from jax.experimental.pallas import tpu as pltpu
from jax.sharding import PartitionSpec as P

MESH = pl.DeviceIdType.MESH
GROUPS = 3
NY = 64
LANES = 128


def kernel(
    sizes,
    forward,
    adjoint,
    log_sigma,
    charge,
    log_tau,
    exponent,
    active,
    source_group,
    group_weight,
    frequency_index,
    prior_weight,
    out,
    own,
    rows,
    from_prev,
    from_next,
    params,
    partial,
    arrived,
    centre,
    around,
    derivs,
    yz_corr,
    yz_grad,
    load_sem,
    halo_send,
    halo_recv,
    gather_sem,
    scatter_sem,
    near_send,
    near_recv,
):
    n_src, n_freq, n_space, count = sizes
    chunks = n_src * n_freq
    half = 2 * chunks
    others = chunks - 1
    s, h, b = lax.axis_index("src"), lax.axis_index("freq"), lax.axis_index("space")
    k = s * n_freq + h
    f32 = jnp.float32

    def device(block, chunk):
        return (chunk // n_freq, lax.rem(chunk, n_freq), block)

    loads = [
        pltpu.make_async_copy(field, own.at[i], load_sem.at[i])
        for i, field in enumerate((forward, adjoint))
    ]
    for load in loads:
        load.start()

    has_prev, has_next = b > 0, b < n_space - 1
    has_low, has_high = k > 0, k < chunks - 1
    near = []
    for db in (-1, 0, 1):
        for dk in (-1, 0, 1):
            if db == 0 and dk == 0:
                continue
            there = True
            if db != 0:
                there = has_prev if db < 0 else has_next
            if dk != 0:
                ok = has_low if dk < 0 else has_high
                there = ok if there is True else jnp.logical_and(there, ok)
            near.append((db, dk, there))

    barrier = pltpu.get_barrier_semaphore()

    def greet(i, carry):
        pl.semaphore_signal(
            barrier, inc=1, device_id=device(b, lax.rem(k + 1 + i, chunks)), device_id_type=MESH
        )
        return carry

    lax.fori_loop(0, others, greet, 0)
    expected = jnp.int32(others)
    for db, dk, there in near:
        if db == 0:
            continue

        @pl.when(there)
        def _():
            pl.semaphore_signal(barrier, inc=1, device_id=device(b + db, k + dk), device_id_type=MESH)

        expected = expected + there.astype(jnp.int32)

    mine = pl.ds(pl.multiple_of(8 * k, 8), 8)
    params[mine, :] = jnp.concatenate(
        [log_sigma[...], charge[...], log_tau[...], exponent[...]], axis=0
    )

    for load in loads:
        load.wait()

    def split_rows(f, carry):
        for i in range(2):
            for r in range(2):
                rows[r, f, pl.ds(half * i, half), :] = own[i, f, pl.ds(r, half, stride=2), :]
        return carry

    lax.fori_loop(0, count, split_rows, 0)

    @pl.when(jnp.logical_not(has_prev))
    def _():
        from_prev[...] = jnp.zeros_like(from_prev)

    @pl.when(jnp.logical_not(has_next))
    def _():
        from_next[...] = jnp.zeros_like(from_next)

    for db, dk, there in near:
        slot = (db + 1) * 3 + dk + 1

        @pl.when(jnp.logical_not(there))
        def _():
            around[slot] = jnp.zeros((8, LANES), f32)

    pl.semaphore_wait(barrier, expected)

    def up(f):
        return pltpu.make_async_remote_copy(
            src_ref=rows.at[1, f],
            dst_ref=from_prev.at[f],
            send_sem=halo_send.at[0, f],
            recv_sem=halo_recv.at[0, f],
            device_id=device(b + 1, k),
            device_id_type=MESH,
        )

    def down(f):
        return pltpu.make_async_remote_copy(
            src_ref=rows.at[0, f],
            dst_ref=from_next.at[f],
            send_sem=halo_send.at[1, f],
            recv_sem=halo_recv.at[1, f],
            device_id=device(b - 1, k),
            device_id_type=MESH,
        )

    def send_halo(f, carry):
        @pl.when(has_next)
        def _():
            up(f).start()

        @pl.when(has_prev)
        def _():
            down(f).start()

        return carry

    lax.fori_loop(0, count, send_halo, 0)

    def send_params(i, carry):
        pltpu.make_async_remote_copy(
            src_ref=params.at[mine],
            dst_ref=params.at[mine],
            send_sem=gather_sem.at[0],
            recv_sem=gather_sem.at[1],
            device_id=device(b, lax.rem(k + 1 + i, chunks)),
            device_id_type=MESH,
        ).start()
        return carry

    lax.fori_loop(0, others, send_params, 0)

    lane = lax.broadcasted_iota(jnp.int32, (chunks, LANES), 1)
    line = lax.broadcasted_iota(jnp.int32, (chunks, LANES), 0)
    low = lane < NY
    y_pos = jnp.bitwise_and(lane, NY - 1)
    y_last, y_first = y_pos == NY - 1, y_pos == 0
    z_last, z_first = line == chunks - 1, line == 0

    def differences(u):
        grad_y = jnp.where(y_last, 0.0, pltpu.roll(u, LANES - 1, 1)) - jnp.where(
            y_first, 0.0, pltpu.roll(u, 1, 1)
        )
        turned = pltpu.roll(u, NY, 1)
        above = jnp.where(z_last, 0.0, pltpu.roll(turned, chunks - 1, 0))
        below = jnp.where(z_first, 0.0, pltpu.roll(turned, 1, 0))
        return grad_y, jnp.where(low, turned - below, above - turned)

    def correlate_yz(f, carry):
        for r in range(2):
            grads = [
                differences(rows[r, f, pl.ds(chunks * i, chunks), :]) for i in range(4)
            ]
            (fr_y, fr_z), (fi_y, fi_z), (ar_y, ar_z), (ai_y, ai_z) = grads
            yz_corr[f, r, 0] = fr_y * ar_y - fi_y * ai_y + (fr_z * ar_z - fi_z * ai_z)
            yz_corr[f, r, 1] = fr_y * ai_y + fi_y * ar_y + (fr_z * ai_z + fi_z * ar_z)
        return carry

    lax.fori_loop(0, count, correlate_yz, 0)

    all_tiles = pl.ds(0, 8 * others)
    gathered = pltpu.make_async_remote_copy(
        src_ref=arrived.at[all_tiles],
        dst_ref=params.at[all_tiles],
        send_sem=gather_sem.at[0],
        recv_sem=gather_sem.at[1],
        device_id=device(b, lax.rem(k + 1, chunks)),
        device_id_type=MESH,
    )
    gathered.wait_recv()

    weight = jnp.float32(0.0)
    for g in range(GROUPS):
        weight = weight + jnp.where(source_group[0] == g, group_weight[g], 0.0)
    scale = weight * (0.25 / math.sqrt(n_src * n_freq * count))

    for r in range(2):
        sigma, chg, tau, expo = (
            params[pl.ds(2 * p + r, chunks, stride=8), :] for p in range(4)
        )
        sigma = jnp.exp(sigma) * scale
        angle = expo * (0.5 * math.pi)
        cosine, sine = jnp.cos(angle), jnp.sin(angle)
        rest = 1.0 - chg
        q_scale = sigma * chg

        def chain(f, totals):
            index = frequency_index[h * count + f].astype(f32)
            log_omega = math.log(2.0 * math.pi) + math.log(10.0) * (
                -1.0 + (4.0 / (n_freq * count - 1)) * index
            )
            log_product = log_omega + tau
            amplitude = jnp.exp(expo * log_product)
            z_r, z_i = amplitude * cosine, amplitude * sine
            d_r, d_i = 1.0 + rest * z_r, rest * z_i
            inverse = 1.0 / (d_r * d_r + d_i * d_i)
            r_r, r_i = d_r * inverse, -d_i * inverse
            s_r, s_i = (1.0 + z_r) * r_r - z_i * r_i, (1.0 + z_r) * r_i + z_i * r_r
            t_r, t_i = z_r * r_r - z_i * r_i, z_r * r_i + z_i * r_r
            s_r, s_i = sigma * s_r, sigma * s_i
            q_r, q_i = q_scale * (t_r * r_r - t_i * r_i), q_scale * (t_r * r_i + t_i * r_r)
            parts = (
                (s_r, s_i),
                (s_r * t_r - s_i * t_i, s_r * t_i + s_i * t_r),
                (expo * q_r, expo * q_i),
                (
                    q_r * log_product - (0.5 * math.pi) * q_i,
                    (0.5 * math.pi) * q_r + q_i * log_product,
                ),
            )
            c_r, c_i = yz_corr[f, r, 0], yz_corr[f, r, 1]
            new = []
            for p, (part_r, part_i) in enumerate(parts):
                derivs[f, r, 2 * p] = part_r
                derivs[f, r, 2 * p + 1] = part_i
                new.append(totals[p] + (part_r * c_r - part_i * c_i))
            return tuple(new)

        zeros = jnp.zeros((chunks, LANES), f32)
        totals = lax.fori_loop(0, count, chain, (zeros,) * 4)
        for p in range(4):
            yz_grad[r, p] = totals[p]

    def add_x(f, totals):
        @pl.when(has_prev)
        def _():
            up(f).wait_recv()

        @pl.when(has_next)
        def _():
            down(f).wait_recv()

        new = []
        for r in range(2):
            ahead = rows.at[1, f] if r == 0 else from_next.at[f]
            behind = from_prev.at[f] if r == 0 else rows.at[0, f]
            f_r, f_i, a_r, a_i = (
                ahead[pl.ds(chunks * i, chunks), :] - behind[pl.ds(chunks * i, chunks), :]
                for i in range(4)
            )
            c_r, c_i = f_r * a_r - f_i * a_i, f_r * a_i + f_i * a_r
            for p in range(4):
                new.append(
                    totals[4 * r + p] + (derivs[f, r, 2 * p] * c_r - derivs[f, r, 2 * p + 1] * c_i)
                )
        return tuple(new)

    totals = lax.fori_loop(
        0, count, add_x, tuple(yz_grad[r, p] for r in range(2) for p in range(4))
    )
    for r in range(2):
        for p in range(4):
            partial[pl.ds(2 * p + r, chunks, stride=8), :] = totals[4 * r + p]

    def send_partial(i, carry):
        target = lax.rem(k + 1 + i, chunks)
        pltpu.make_async_remote_copy(
            src_ref=partial.at[pl.ds(pl.multiple_of(8 * target, 8), 8)],
            dst_ref=arrived.at[pl.ds(pl.multiple_of(8 * i, 8), 8)],
            send_sem=scatter_sem.at[0],
            recv_sem=scatter_sem.at[1],
            device_id=device(b, target),
            device_id_type=MESH,
        ).start()
        return carry

    lax.fori_loop(0, others, send_partial, 0)
    mask = jnp.concatenate([active[...].astype(f32)] * 4, axis=0)
    scattered = pltpu.make_async_remote_copy(
        src_ref=partial.at[all_tiles],
        dst_ref=arrived.at[all_tiles],
        send_sem=scatter_sem.at[0],
        recv_sem=scatter_sem.at[1],
        device_id=device(b, lax.rem(k + 1, chunks)),
        device_id_type=MESH,
    )
    scattered.wait_recv()
    tiles = [partial[mine, :]] + [arrived[pl.ds(8 * i, 8), :] for i in range(others)]
    while len(tiles) > 1:
        tiles = [
            tiles[i] + tiles[i + 1] if i + 1 < len(tiles) else tiles[i]
            for i in range(0, len(tiles), 2)
        ]
    masked = tiles[0] * mask
    centre[...] = masked

    def to_near(db, dk):
        slot = (1 - db) * 3 + 1 - dk
        return pltpu.make_async_remote_copy(
            src_ref=centre,
            dst_ref=around.at[slot],
            send_sem=near_send.at[slot],
            recv_sem=near_recv.at[slot],
            device_id=device(b + db, k + dk),
            device_id_type=MESH,
        )

    for db, dk, there in near:

        @pl.when(there)
        def _():
            to_near(db, dk).start()

    tile_lane = lax.broadcasted_iota(jnp.int32, (8, LANES), 1)
    tile_line = lax.broadcasted_iota(jnp.int32, (8, LANES), 0)
    tile_low = tile_lane < NY
    tile_y = jnp.bitwise_and(tile_lane, NY - 1)
    top, bottom = tile_y == NY - 1, tile_y == 0
    first_row = jnp.bitwise_and(tile_line, 1) == 0
    smooth = []
    for d in range(3):
        w = jnp.full((8, LANES), prior_weight[0, d], f32)
        for p in range(1, 4):
            w = jnp.where(tile_line >= 2 * p, prior_weight[p, d], w)
        smooth.append(w)

    def one_pass(mid, prev, after, lower, upper):
        x_sum = jnp.where(first_row, pltpu.roll(mid, 7, 0), pltpu.roll(after, 1, 0)) + jnp.where(
            first_row, pltpu.roll(prev, 7, 0), pltpu.roll(mid, 1, 0)
        )
        y_sum = jnp.where(top, 0.0, pltpu.roll(mid, LANES - 1, 1)) + jnp.where(
            bottom, 0.0, pltpu.roll(mid, 1, 1)
        )
        turned = pltpu.roll(mid, NY, 1)
        z_sum = jnp.where(tile_low, turned, pltpu.roll(upper, NY, 1)) + jnp.where(
            tile_low, pltpu.roll(lower, NY, 1), turned
        )
        twice = 2.0 * mid
        return (
            mid
            + smooth[0] * (x_sum - twice)
            + smooth[1] * (y_sum - twice)
            + smooth[2] * (z_sum - twice)
        )

    for db, dk, there in near:

        @pl.when(there)
        def _():
            to_near(-db, -dk).wait_recv()

    def tile(db, dk):
        return masked if db == 0 and dk == 0 else around[(db + 1) * 3 + dk + 1]

    empty = jnp.zeros((8, LANES), f32)

    def inside(there, value):
        return jnp.where(there, value, 0.0)

    mid = one_pass(masked, tile(-1, 0), tile(1, 0), tile(0, -1), tile(0, 1))
    prev = one_pass(tile(-1, 0), empty, masked, tile(-1, -1), tile(-1, 1))
    after = one_pass(tile(1, 0), masked, empty, tile(1, -1), tile(1, 1))
    lower = one_pass(tile(0, -1), tile(-1, -1), tile(1, -1), empty, masked)
    upper = one_pass(tile(0, 1), tile(-1, 1), tile(1, 1), masked, empty)
    out[...] = one_pass(
        mid,
        inside(has_prev, prev),
        inside(has_next, after),
        inside(has_low, lower),
        inside(has_high, upper),
    )

    def sent_halo(f, carry):
        @pl.when(has_next)
        def _():
            up(f).wait_send()

        @pl.when(has_prev)
        def _():
            down(f).wait_send()

        return carry

    lax.fori_loop(0, count, sent_halo, 0)
    gathered.wait_send()
    scattered.wait_send()
    for db, dk, there in near:

        @pl.when(there)
        def _():
            to_near(db, dk).wait_send()


def solution(mesh):
    n_src, n_freq, n_space = mesh.shape["src"], mesh.shape["freq"], mesh.shape["space"]
    chunks = n_src * n_freq

    def local(
        forward,
        adjoint,
        source_group,
        group_weight,
        frequency_index,
        log_sigma,
        charge,
        log_tau,
        exponent,
        active,
        prior_weight,
    ):
        count = forward.shape[1]

        def lines(field):
            split = field.reshape(count, 2, 2, chunks, LANES)
            return split.transpose(0, 1, 3, 2, 4).reshape(count, 4 * chunks, LANES)

        any_spec = pl.BlockSpec(memory_space=pl.ANY)
        vmem = pl.BlockSpec(memory_space=pltpu.VMEM)
        smem = pl.BlockSpec(memory_space=pltpu.SMEM)
        f32 = jnp.float32
        result = pl.pallas_call(
            functools.partial(kernel, (n_src, n_freq, n_space, count)),
            out_shape=jax.ShapeDtypeStruct((8, LANES), f32),
            in_specs=[any_spec] * 2 + [vmem] * 5 + [smem] * 4,
            out_specs=vmem,
            scratch_shapes=[
                pltpu.VMEM((2, count, 4 * chunks, LANES), f32),
                pltpu.VMEM((2, count, 4 * chunks, LANES), f32),
                pltpu.VMEM((count, 4 * chunks, LANES), f32),
                pltpu.VMEM((count, 4 * chunks, LANES), f32),
                pltpu.VMEM((8 * chunks, LANES), f32),
                pltpu.VMEM((8 * chunks, LANES), f32),
                pltpu.VMEM((8 * chunks, LANES), f32),
                pltpu.VMEM((8, LANES), f32),
                pltpu.VMEM((9, 8, LANES), f32),
                pltpu.VMEM((count, 2, 8, chunks, LANES), f32),
                pltpu.VMEM((count, 2, 2, chunks, LANES), f32),
                pltpu.VMEM((2, 4, chunks, LANES), f32),
                pltpu.SemaphoreType.DMA((2,)),
                pltpu.SemaphoreType.DMA((2, count)),
                pltpu.SemaphoreType.DMA((2, count)),
                pltpu.SemaphoreType.DMA((2,)),
                pltpu.SemaphoreType.DMA((2,)),
                pltpu.SemaphoreType.DMA((9,)),
                pltpu.SemaphoreType.DMA((9,)),
            ],
            compiler_params=pltpu.CompilerParams(
                collective_id=0, has_side_effects=True, vmem_limit_bytes=32 * 1024 * 1024
            ),
        )(
            lines(forward),
            lines(adjoint),
            log_sigma,
            charge,
            log_tau,
            exponent,
            active,
            source_group,
            group_weight,
            frequency_index,
            prior_weight,
        )
        return result.reshape(4, 2, LANES)

    placed = (
        P("src", "freq", None, "space", None),
        P("src", "freq", None, "space", None),
        P("src"),
        P(),
        P(),
        P("space", ("src", "freq")),
        P("space", ("src", "freq")),
        P("space", ("src", "freq")),
        P("space", ("src", "freq")),
        P("space", ("src", "freq")),
        P(),
    )
    return jax.shard_map(
        local,
        mesh=mesh,
        in_specs=placed,
        out_specs=P(None, "space", ("src", "freq")),
        check_vma=False,
    )
```

```python
import functools
import math

import jax
import jax.numpy as jnp
from jax import lax
from jax.experimental import pallas as pl
from jax.experimental.pallas import tpu as pltpu
from jax.sharding import PartitionSpec as P

MESH = pl.DeviceIdType.MESH
GROUPS = 3
NY = 64
LANES = 128


def kernel(
    sizes,
    forward,
    adjoint,
    log_sigma,
    charge,
    log_tau,
    exponent,
    active_in,
    source_group,
    group_weight,
    frequency_index,
    prior_weight,
    out,
    cell_params,
    active,
    own,
    rows,
    from_prev,
    from_next,
    params,
    masks,
    partial,
    arrived,
    window,
    derivs,
    yz_corr,
    yz_grad,
    load_sem,
    small_sem,
    halo_send,
    halo_recv,
    pair_send,
    pair_recv,
    gather_sem,
    scatter_sem,
    near_send,
    near_recv,
):
    n_src, n_space, count = sizes
    chunks = 2 * n_src
    half = 2 * chunks
    s, h, b = lax.axis_index("src"), lax.axis_index("freq"), lax.axis_index("space")
    k = 2 * s + h
    f32 = jnp.float32
    steps = sorted(range(1, n_src), key=lambda step: -min(step, n_src - step))

    def along(step):
        return lax.rem(s + step, n_src)

    loads = [
        pltpu.make_async_copy(field, own.at[i], load_sem.at[i])
        for i, field in enumerate((forward, adjoint))
    ]
    small = [
        pltpu.make_async_copy(source, target, small_sem.at[i])
        for i, (source, target) in enumerate(
            (
                (log_sigma, cell_params.at[0]),
                (charge, cell_params.at[1]),
                (log_tau, cell_params.at[2]),
                (exponent, cell_params.at[3]),
                (active_in, active),
            )
        )
    ]
    for load in loads + small:
        load.start()

    has_prev, has_next = b > 0, b < n_space - 1
    beside = {-1: has_prev, 0: None, 1: has_next}

    def both(first, second):
        if first is None or second is None:
            return second if first is None else first
        return jnp.logical_and(first, second)

    def in_window(slot, share, start, size):
        return pl.ds(pl.multiple_of(48 * slot + 24 * share + start, 8), size)

    def where_there(there, act):
        if there is None:
            act()
        else:
            pl.when(there)(act)

    side, away = s - 1 + 2 * h, s + 1 - 2 * h
    has_side = jnp.logical_and(side >= 0, side < n_src)
    has_away = jnp.logical_and(away >= 0, away < n_src)
    sends = []
    for db in (-1, 0, 1):
        if db != 0:
            sends.append((beside[db], 0, (s, h, b + db), (8 - 8 * h, 16), 1 - db, 0))
        sends.append((beside[db], 0, (s, 1 - h, b + db), (8 * h, 16), 1 - db, 0))
        there = both(has_away, beside[db])
        sends.append((there, 8 - 8 * h, (away, h, b + db), (16 * h, 8), 1 - db, 1))
        there = both(has_side, beside[db])
        sends.append((there, 8 * h, (side, 1 - h, b + db), (16 - 16 * h, 8), 1 - db, 1))
    receives = []
    for db in (-1, 0, 1):
        if db != 0:
            receives.append((beside[db], (s, h, b + db), (8 - 8 * h, 16), 1 + db, h, 0))
        receives.append((beside[db], (s, 1 - h, b + db), (8 - 8 * h, 16), 1 + db, 1 - h, 0))
        for other in (h, 1 - h):
            there = both(has_side, beside[db])
            receives.append((there, (side, other, b + db), (16 * h, 8), 1 + db, other, 1))

    barrier = pltpu.get_barrier_semaphore()

    def greet(device):
        pl.semaphore_signal(barrier, inc=1, device_id=device, device_id_type=MESH)

    for there, device, _, slot, other, kind in receives:
        if kind == 1 and slot == 1 and other is h:
            continue
        where_there(there, functools.partial(greet, device))
    for step in steps:
        greet((along(step), h, b))
    one = jnp.int32(1)
    sides = has_prev.astype(jnp.int32) + has_next.astype(jnp.int32)
    expected = n_src - 1 + one + 2 * sides
    expected = expected + has_side.astype(jnp.int32) * (1 + sides)
    expected = expected + has_away.astype(jnp.int32) * sides

    mine = pl.ds(pl.multiple_of(8 * k, 8), 8)
    my_half = pl.ds(pl.multiple_of(8 * h, 8), 8)
    for load in small:
        load.wait()
    params[mine, :] = jnp.concatenate([cell_params[p] for p in range(4)], axis=0)
    masks[my_half, :] = jnp.concatenate([active[...].astype(f32)] * 4, axis=0)

    for load in loads:
        load.wait()

    def split_rows(f, carry):
        for i in range(2):
            for r in range(2):
                rows[r, f, pl.ds(half * i, half), :] = own[i, f, pl.ds(r, half, stride=2), :]
        return carry

    lax.fori_loop(0, count, split_rows, 0)

    @pl.when(jnp.logical_not(has_prev))
    def _():
        from_prev[...] = jnp.zeros_like(from_prev)
        window[pl.ds(0, 48), :] = jnp.zeros((48, LANES), f32)

    @pl.when(jnp.logical_not(has_next))
    def _():
        from_next[...] = jnp.zeros_like(from_next)
        window[pl.ds(96, 48), :] = jnp.zeros((48, LANES), f32)

    @pl.when(jnp.logical_not(has_side))
    def _():
        for db in range(3):
            for other in range(2):
                window[in_window(db, other, 16 * h, 8), :] = jnp.zeros((8, LANES), f32)

    pl.semaphore_wait(barrier, expected)

    def to_partner(i):
        ref, part = ((params, mine), (masks, my_half))[i]
        return pltpu.make_async_remote_copy(
            src_ref=ref.at[part],
            dst_ref=ref.at[part],
            send_sem=pair_send.at[i],
            recv_sem=pair_recv.at[i],
            device_id=(s, 1 - h, b),
            device_id_type=MESH,
        )

    to_partner(0).start()

    def up(f):
        return pltpu.make_async_remote_copy(
            src_ref=rows.at[1, f],
            dst_ref=from_prev.at[f],
            send_sem=halo_send.at[0, f],
            recv_sem=halo_recv.at[0, f],
            device_id=(s, h, b + 1),
            device_id_type=MESH,
        )

    def down(f):
        return pltpu.make_async_remote_copy(
            src_ref=rows.at[0, f],
            dst_ref=from_next.at[f],
            send_sem=halo_send.at[1, f],
            recv_sem=halo_recv.at[1, f],
            device_id=(s, h, b - 1),
            device_id_type=MESH,
        )

    def send_halo(f, carry):
        @pl.when(has_next)
        def _():
            up(f).start()

        @pl.when(has_prev)
        def _():
            down(f).start()

        return carry

    lax.fori_loop(0, count, send_halo, 0)
    to_partner(1).start()

    lane = lax.broadcasted_iota(jnp.int32, (chunks, LANES), 1)
    line = lax.broadcasted_iota(jnp.int32, (chunks, LANES), 0)
    low = lane < NY
    y_pos = jnp.bitwise_and(lane, NY - 1)
    y_last, y_first = y_pos == NY - 1, y_pos == 0
    z_last, z_first = line == chunks - 1, line == 0

    def differences(u):
        grad_y = jnp.where(y_last, 0.0, pltpu.roll(u, LANES - 1, 1)) - jnp.where(
            y_first, 0.0, pltpu.roll(u, 1, 1)
        )
        turned = pltpu.roll(u, NY, 1)
        above = jnp.where(z_last, 0.0, pltpu.roll(turned, chunks - 1, 0))
        below = jnp.where(z_first, 0.0, pltpu.roll(turned, 1, 0))
        return grad_y, jnp.where(low, turned - below, above - turned)

    def correlate_yz(f, carry):
        for r in range(2):
            grads = [
                differences(rows[r, f, pl.ds(chunks * i, chunks), :]) for i in range(4)
            ]
            (fr_y, fr_z), (fi_y, fi_z), (ar_y, ar_z), (ai_y, ai_z) = grads
            yz_corr[f, r, 0] = fr_y * ar_y - fi_y * ai_y + (fr_z * ar_z - fi_z * ai_z)
            yz_corr[f, r, 1] = fr_y * ai_y + fi_y * ar_y + (fr_z * ai_z + fi_z * ar_z)
        return carry

    lax.fori_loop(0, count, correlate_yz, 0)

    to_partner(0).wait_recv()
    pair = pl.ds(pl.multiple_of(16 * s, 16), 16)
    for step in steps:
        pltpu.make_async_remote_copy(
            src_ref=params.at[pair],
            dst_ref=params.at[pair],
            send_sem=gather_sem.at[0],
            recv_sem=gather_sem.at[1],
            device_id=(along(step), h, b),
            device_id_type=MESH,
        ).start()
    others = pl.ds(0, 16 * (n_src - 1))
    gathered = pltpu.make_async_remote_copy(
        src_ref=partial.at[others],
        dst_ref=params.at[others],
        send_sem=gather_sem.at[0],
        recv_sem=gather_sem.at[1],
        device_id=(along(1), h, b),
        device_id_type=MESH,
    )
    gathered.wait_recv()

    weight = jnp.float32(0.0)
    for g in range(GROUPS):
        weight = weight + jnp.where(source_group[0] == g, group_weight[g], 0.0)
    scale = weight * (0.25 / math.sqrt(n_src * 2 * count))

    for r in range(2):
        sigma, chg, tau, expo = (
            params[pl.ds(2 * p + r, chunks, stride=8), :] for p in range(4)
        )
        sigma = jnp.exp(sigma) * scale
        angle = expo * (0.5 * math.pi)
        cosine, sine = jnp.cos(angle), jnp.sin(angle)
        rest = 1.0 - chg
        q_scale = sigma * chg

        def chain(f, totals):
            index = frequency_index[h * count + f].astype(f32)
            log_omega = math.log(2.0 * math.pi) + math.log(10.0) * (
                -1.0 + (4.0 / (2 * count - 1)) * index
            )
            log_product = log_omega + tau
            amplitude = jnp.exp(expo * log_product)
            z_r, z_i = amplitude * cosine, amplitude * sine
            d_r, d_i = 1.0 + rest * z_r, rest * z_i
            inverse = 1.0 / (d_r * d_r + d_i * d_i)
            r_r, r_i = d_r * inverse, -d_i * inverse
            s_r, s_i = (1.0 + z_r) * r_r - z_i * r_i, (1.0 + z_r) * r_i + z_i * r_r
            t_r, t_i = z_r * r_r - z_i * r_i, z_r * r_i + z_i * r_r
            s_r, s_i = sigma * s_r, sigma * s_i
            q_r, q_i = q_scale * (t_r * r_r - t_i * r_i), q_scale * (t_r * r_i + t_i * r_r)
            parts = (
                (s_r, s_i),
                (s_r * t_r - s_i * t_i, s_r * t_i + s_i * t_r),
                (expo * q_r, expo * q_i),
                (
                    q_r * log_product - (0.5 * math.pi) * q_i,
                    (0.5 * math.pi) * q_r + q_i * log_product,
                ),
            )
            c_r, c_i = yz_corr[f, r, 0], yz_corr[f, r, 1]
            new = []
            for p, (part_r, part_i) in enumerate(parts):
                derivs[f, r, 2 * p] = part_r
                derivs[f, r, 2 * p + 1] = part_i
                new.append(totals[p] + (part_r * c_r - part_i * c_i))
            return tuple(new)

        zeros = jnp.zeros((chunks, LANES), f32)
        totals = lax.fori_loop(0, count, chain, (zeros,) * 4)
        for p in range(4):
            yz_grad[r, p] = totals[p]

    def add_x(f, totals):
        @pl.when(has_prev)
        def _():
            up(f).wait_recv()

        @pl.when(has_next)
        def _():
            down(f).wait_recv()

        new = []
        for r in range(2):
            ahead = rows.at[1, f] if r == 0 else from_next.at[f]
            behind = from_prev.at[f] if r == 0 else rows.at[0, f]
            f_r, f_i, a_r, a_i = (
                ahead[pl.ds(chunks * i, chunks), :] - behind[pl.ds(chunks * i, chunks), :]
                for i in range(4)
            )
            c_r, c_i = f_r * a_r - f_i * a_i, f_r * a_i + f_i * a_r
            for p in range(4):
                new.append(
                    totals[4 * r + p] + (derivs[f, r, 2 * p] * c_r - derivs[f, r, 2 * p + 1] * c_i)
                )
        return tuple(new)

    totals = lax.fori_loop(
        0, count, add_x, tuple(yz_grad[r, p] for r in range(2) for p in range(4))
    )
    for r in range(2):
        for p in range(4):
            partial[pl.ds(2 * p + r, chunks, stride=8), :] = totals[4 * r + p]

    for i, step in enumerate(steps):
        to = along(step)
        pltpu.make_async_remote_copy(
            src_ref=partial.at[pl.ds(pl.multiple_of(16 * to, 16), 16)],
            dst_ref=arrived.at[pl.ds(16 * i, 16)],
            send_sem=scatter_sem.at[0],
            recv_sem=scatter_sem.at[1],
            device_id=(to, h, b),
            device_id_type=MESH,
        ).start()
    to_partner(1).wait_recv()
    mask = masks[...]
    scattered = pltpu.make_async_remote_copy(
        src_ref=partial.at[others],
        dst_ref=arrived.at[others],
        send_sem=scatter_sem.at[0],
        recv_sem=scatter_sem.at[1],
        device_id=(along(1), h, b),
        device_id_type=MESH,
    )
    scattered.wait_recv()
    tiles = [partial[pair, :]] + [arrived[pl.ds(16 * i, 16), :] for i in range(n_src - 1)]
    while len(tiles) > 1:
        tiles = [
            tiles[i] + tiles[i + 1] if i + 1 < len(tiles) else tiles[i]
            for i in range(0, len(tiles), 2)
        ]
    window[in_window(1, h, 8 - 8 * h, 16), :] = tiles[0] * mask

    def to_near(entry):
        there, part, device, (start, size), slot, kind = sends[entry]
        return pltpu.make_async_remote_copy(
            src_ref=window.at[in_window(1, h, 8 - 8 * h + part, size)],
            dst_ref=window.at[in_window(slot, h, start, size)],
            send_sem=near_send.at[entry],
            recv_sem=near_recv.at[4 * slot + 2 * h + kind],
            device_id=device,
            device_id_type=MESH,
        )

    def from_near(entry):
        there, device, (start, size), slot, other, kind = receives[entry]
        part = window.at[in_window(slot, other, start, size)]
        return pltpu.make_async_remote_copy(
            src_ref=part,
            dst_ref=part,
            send_sem=near_send.at[0],
            recv_sem=near_recv.at[4 * slot + 2 * other + kind],
            device_id=device,
            device_id_type=MESH,
        )

    for entry in range(len(sends)):
        where_there(sends[entry][0], lambda entry=entry: to_near(entry).start())

    tile_lane = lax.broadcasted_iota(jnp.int32, (8, LANES), 1)
    tile_line = lax.broadcasted_iota(jnp.int32, (8, LANES), 0)
    tile_low = tile_lane < NY
    tile_y = jnp.bitwise_and(tile_lane, NY - 1)
    top, bottom = tile_y == NY - 1, tile_y == 0
    first_row = jnp.bitwise_and(tile_line, 1) == 0
    smooth = []
    for d in range(3):
        w = jnp.full((8, LANES), prior_weight[0, d], f32)
        for p in range(1, 4):
            w = jnp.where(tile_line >= 2 * p, prior_weight[p, d], w)
        smooth.append(w)

    def one_pass(mid, prev, after, lower, upper):
        x_sum = jnp.where(first_row, pltpu.roll(mid, 7, 0), pltpu.roll(after, 1, 0)) + jnp.where(
            first_row, pltpu.roll(prev, 7, 0), pltpu.roll(mid, 1, 0)
        )
        y_sum = jnp.where(top, 0.0, pltpu.roll(mid, LANES - 1, 1)) + jnp.where(
            bottom, 0.0, pltpu.roll(mid, 1, 1)
        )
        turned = pltpu.roll(mid, NY, 1)
        z_sum = jnp.where(tile_low, turned, pltpu.roll(upper, NY, 1)) + jnp.where(
            tile_low, pltpu.roll(lower, NY, 1), turned
        )
        twice = 2.0 * mid
        return (
            mid
            + smooth[0] * (x_sum - twice)
            + smooth[1] * (y_sum - twice)
            + smooth[2] * (z_sum - twice)
        )

    for entry in range(len(receives)):
        where_there(receives[entry][0], lambda entry=entry: from_near(entry).wait_recv())

    def tile(db, dk):
        return sum(window[in_window(db + 1, other, 8 * (dk + 1), 8), :] for other in range(2))

    empty = jnp.zeros((8, LANES), f32)

    def inside(there, value):
        return jnp.where(there, value, 0.0)

    middle = tile(0, 0)
    mid = one_pass(middle, tile(-1, 0), tile(1, 0), tile(0, -1), tile(0, 1))
    prev = one_pass(tile(-1, 0), empty, middle, tile(-1, -1), tile(-1, 1))
    after = one_pass(tile(1, 0), middle, empty, tile(1, -1), tile(1, 1))
    lower = one_pass(tile(0, -1), tile(-1, -1), tile(1, -1), empty, middle)
    upper = one_pass(tile(0, 1), tile(-1, 1), tile(1, 1), middle, empty)
    out[...] = one_pass(
        mid,
        inside(has_prev, prev),
        inside(has_next, after),
        inside(k > 0, lower),
        inside(k < chunks - 1, upper),
    )

    def sent_halo(f, carry):
        @pl.when(has_next)
        def _():
            up(f).wait_send()

        @pl.when(has_prev)
        def _():
            down(f).wait_send()

        return carry

    lax.fori_loop(0, count, sent_halo, 0)
    to_partner(0).wait_send()
    to_partner(1).wait_send()
    gathered.wait_send()
    scattered.wait_send()
    for entry in range(len(sends)):
        where_there(sends[entry][0], lambda entry=entry: to_near(entry).wait_send())


def solution(mesh):
    n_src, n_space = mesh.shape["src"], mesh.shape["space"]
    chunks = 2 * n_src

    def local(
        forward,
        adjoint,
        source_group,
        group_weight,
        frequency_index,
        log_sigma,
        charge,
        log_tau,
        exponent,
        active,
        prior_weight,
    ):
        count = forward.shape[1]

        def keep(x):
            return pltpu.with_memory_space_constraint(x, pltpu.HBM)

        def lines(field):
            split = field.reshape(count, 2, 2, chunks, LANES)
            return split.transpose(0, 1, 3, 2, 4).reshape(count, 4 * chunks, LANES)

        hbm = pl.BlockSpec(memory_space=pl.ANY)
        vmem = pl.BlockSpec(memory_space=pltpu.VMEM)
        smem = pl.BlockSpec(memory_space=pltpu.SMEM)
        f32 = jnp.float32
        result = pl.pallas_call(
            functools.partial(kernel, (n_src, n_space, count)),
            out_shape=jax.ShapeDtypeStruct((8, LANES), f32),
            in_specs=[hbm] * 7 + [smem] * 4,
            out_specs=vmem,
            scratch_shapes=[
                pltpu.VMEM((4, 2, LANES), f32),
                pltpu.VMEM((2, LANES), jnp.int32),
                pltpu.VMEM((2, count, 4 * chunks, LANES), f32),
                pltpu.VMEM((2, count, 4 * chunks, LANES), f32),
                pltpu.VMEM((count, 4 * chunks, LANES), f32),
                pltpu.VMEM((count, 4 * chunks, LANES), f32),
                pltpu.VMEM((8 * chunks, LANES), f32),
                pltpu.VMEM((16, LANES), f32),
                pltpu.VMEM((8 * chunks, LANES), f32),
                pltpu.VMEM((8 * chunks, LANES), f32),
                pltpu.VMEM((6 * 24, LANES), f32),
                pltpu.VMEM((count, 2, 8, chunks, LANES), f32),
                pltpu.VMEM((count, 2, 2, chunks, LANES), f32),
                pltpu.VMEM((2, 4, chunks, LANES), f32),
                pltpu.SemaphoreType.DMA((2,)),
                pltpu.SemaphoreType.DMA((5,)),
                pltpu.SemaphoreType.DMA((2, count)),
                pltpu.SemaphoreType.DMA((2, count)),
                pltpu.SemaphoreType.DMA((2,)),
                pltpu.SemaphoreType.DMA((2,)),
                pltpu.SemaphoreType.DMA((2,)),
                pltpu.SemaphoreType.DMA((2,)),
                pltpu.SemaphoreType.DMA((11,)),
                pltpu.SemaphoreType.DMA((12,)),
            ],
            compiler_params=pltpu.CompilerParams(
                collective_id=0, has_side_effects=True, vmem_limit_bytes=32 * 1024 * 1024
            ),
        )(
            *map(keep, (lines(forward), lines(adjoint), log_sigma, charge, log_tau, exponent, active)),
            source_group,
            *map(keep, (group_weight, frequency_index, prior_weight)),
        )
        return result.reshape(4, 2, LANES)

    placed = (
        P("src", "freq", None, "space", None),
        P("src", "freq", None, "space", None),
        P("src"),
        P(),
        P(),
        P("space", ("src", "freq")),
        P("space", ("src", "freq")),
        P("space", ("src", "freq")),
        P("space", ("src", "freq")),
        P("space", ("src", "freq")),
        P(),
    )
    return jax.shard_map(
        local,
        mesh=mesh,
        in_specs=placed,
        out_specs=P(None, "space", ("src", "freq")),
        check_vma=False,
    )
```

```python
import functools
import math

import jax
import jax.numpy as jnp
from jax import lax
from jax.experimental import pallas as pl
from jax.experimental.pallas import tpu as pltpu
from jax.sharding import PartitionSpec as P

MESH = pl.DeviceIdType.MESH
GROUPS = 3
NY = 64
LANES = 128


def kernel(
    sizes,
    forward,
    adjoint,
    log_sigma,
    charge,
    log_tau,
    exponent,
    active_in,
    source_group,
    group_weight,
    frequency_index,
    prior_weight,
    out,
    cell_params,
    active,
    own,
    rows,
    from_prev,
    from_next,
    params,
    masks,
    partial,
    arrived,
    window,
    derivs,
    yz_corr,
    log_omega,
    load_sem,
    small_sem,
    halo_send,
    halo_recv,
    pair_send,
    pair_recv,
    gather_sem,
    scatter_sem,
    near_send,
    near_recv,
    first_sem,
    second_sem,
):
    n_src, n_space, count = sizes
    chunks = 2 * n_src
    half = 2 * chunks
    size = min(8, chunks)
    groups = chunks // size
    places = size // 2
    s, h, b = lax.axis_index("src"), lax.axis_index("freq"), lax.axis_index("space")
    k = 2 * s + h
    f32 = jnp.float32
    steps = sorted(range(1, n_src), key=lambda step: -min(step, n_src - step))

    def along(step):
        return lax.rem(s + step, n_src)

    loads = [
        pltpu.make_async_copy(field, own.at[i], load_sem.at[i])
        for i, field in enumerate((forward, adjoint))
    ]
    small = [
        pltpu.make_async_copy(source, target, small_sem.at[i])
        for i, (source, target) in enumerate(
            (
                (log_sigma, cell_params.at[0]),
                (charge, cell_params.at[1]),
                (log_tau, cell_params.at[2]),
                (exponent, cell_params.at[3]),
                (active_in, active),
            )
        )
    ]
    for load in loads + small:
        load.start()

    has_prev, has_next = b > 0, b < n_space - 1
    beside = {-1: has_prev, 0: None, 1: has_next}

    def both(first, second):
        if first is None or second is None:
            return second if first is None else first
        return jnp.logical_and(first, second)

    def in_window(slot, share, start, length):
        return pl.ds(pl.multiple_of(48 * slot + 24 * share + start, 8), length)

    def where_there(there, act):
        if there is None:
            act()
        else:
            pl.when(there)(act)

    side, away = s - 1 + 2 * h, s + 1 - 2 * h
    has_side = jnp.logical_and(side >= 0, side < n_src)
    has_away = jnp.logical_and(away >= 0, away < n_src)
    sends = []
    for db in (-1, 0, 1):
        if db != 0:
            sends.append((beside[db], 0, (s, h, b + db), (8 - 8 * h, 16), 1 - db, 0))
        sends.append((beside[db], 0, (s, 1 - h, b + db), (8 * h, 16), 1 - db, 0))
        there = both(has_away, beside[db])
        sends.append((there, 8 - 8 * h, (away, h, b + db), (16 * h, 8), 1 - db, 1))
        there = both(has_side, beside[db])
        sends.append((there, 8 * h, (side, 1 - h, b + db), (16 - 16 * h, 8), 1 - db, 1))
    receives = []
    for db in (-1, 0, 1):
        if db != 0:
            receives.append((beside[db], (s, h, b + db), (8 - 8 * h, 16), 1 + db, h, 0))
        receives.append((beside[db], (s, 1 - h, b + db), (8 - 8 * h, 16), 1 + db, 1 - h, 0))
        for other in (h, 1 - h):
            there = both(has_side, beside[db])
            receives.append((there, (side, other, b + db), (16 * h, 8), 1 + db, other, 1))

    odd = lax.rem(b, 2)
    first_core, second_core = b - odd, b - odd + 1
    next_chip = first_core - 2 + 4 * odd
    has_chip = jnp.logical_and(next_chip >= 0, next_chip < n_space)
    barrier = pltpu.get_barrier_semaphore()

    def greet(*device):
        pl.semaphore_signal(barrier, inc=1, device_id=device, device_id_type=MESH)

    where_there(odd == 1, functools.partial(greet, s, h, first_core))
    where_there(has_chip, functools.partial(greet, s, h, next_chip))
    greet(s, 1 - h, first_core)

    where_there(both(has_side, has_chip), functools.partial(greet, side, 1 - h, next_chip + 1))
    where_there(has_side, functools.partial(greet, side, 1 - h, second_core))
    where_there(has_chip, functools.partial(greet, s, 1 - h, next_chip + 1))
    for step in steps:
        greet(along(step), h, second_core)
    where_there(both(has_side, has_chip), functools.partial(greet, side, h, next_chip + 1))

    chips = (first_core > 0).astype(jnp.int32) + (second_core < n_space - 1).astype(jnp.int32)
    to_side, to_away = has_side.astype(jnp.int32), has_away.astype(jnp.int32)
    first_count = 3 + chips
    second_count = 2 * (n_src - 1) + chips * (1 + to_side + to_away) + 2 * to_side

    mine = pl.ds(pl.multiple_of(8 * k, 8), 8)
    my_half = pl.ds(pl.multiple_of(8 * h, 8), 8)
    for load in small:
        load.wait()
    params[mine, :] = jnp.concatenate([cell_params[p] for p in range(4)], axis=0)
    masks[my_half, :] = jnp.concatenate([active[...].astype(f32)] * 4, axis=0)

    for load in loads:
        load.wait()

    def split_rows(f, carry):
        for i in range(2):
            for r in range(2):
                for c in range(2):
                    first = half * c + r
                    rows[r, f, 2 * i + c] = own[i, f, pl.ds(first, chunks, stride=2), :]
        return carry

    lax.fori_loop(0, count, split_rows, 0)

    @pl.when(jnp.logical_not(has_prev))
    def _():
        from_prev[...] = jnp.zeros_like(from_prev)
        window[pl.ds(0, 48), :] = jnp.zeros((48, LANES), f32)

    @pl.when(jnp.logical_not(has_next))
    def _():
        from_next[...] = jnp.zeros_like(from_next)
        window[pl.ds(96, 48), :] = jnp.zeros((48, LANES), f32)

    @pl.when(jnp.logical_not(has_side))
    def _():
        for db in range(3):
            for other in range(2):
                window[in_window(db, other, 16 * h, 8), :] = jnp.zeros((8, LANES), f32)

    @pl.when(odd == 0)
    def _():
        pl.semaphore_wait(barrier, first_count)
        pl.semaphore_signal(first_sem, inc=1, device_id=(s, h, second_core), device_id_type=MESH)

    @pl.when(odd == 1)
    def _():
        pl.semaphore_wait(first_sem, 1)

    def to_partner(i):
        ref, part = ((params, mine), (masks, my_half))[i]
        return pltpu.make_async_remote_copy(
            src_ref=ref.at[part],
            dst_ref=ref.at[part],
            send_sem=pair_send.at[i],
            recv_sem=pair_recv.at[i],
            device_id=(s, 1 - h, b),
            device_id_type=MESH,
        )

    to_partner(0).start()

    def part(g):
        return pl.ds(size * g, size)

    def up(g):
        return pltpu.make_async_remote_copy(
            src_ref=rows.at[1, :, :, part(g), :],
            dst_ref=from_prev.at[:, :, part(g), :],
            send_sem=halo_send.at[0, g],
            recv_sem=halo_recv.at[0, g],
            device_id=(s, h, b + 1),
            device_id_type=MESH,
        )

    def down(g):
        return pltpu.make_async_remote_copy(
            src_ref=rows.at[0, :, :, part(g), :],
            dst_ref=from_next.at[:, :, part(g), :],
            send_sem=halo_send.at[1, g],
            recv_sem=halo_recv.at[1, g],
            device_id=(s, h, b - 1),
            device_id_type=MESH,
        )

    for g in range(groups):
        where_there(has_next, lambda g=g: up(g).start())
        where_there(has_prev, lambda g=g: down(g).start())
    to_partner(1).start()

    lane = lax.broadcasted_iota(jnp.int32, (chunks, LANES), 1)
    line = lax.broadcasted_iota(jnp.int32, (chunks, LANES), 0)
    low = lane < NY
    y_pos = jnp.bitwise_and(lane, NY - 1)
    y_last, y_first = y_pos == NY - 1, y_pos == 0
    z_last, z_first = line == chunks - 1, line == 0

    def differences(u):
        grad_y = jnp.where(y_last, 0.0, pltpu.roll(u, LANES - 1, 1)) - jnp.where(
            y_first, 0.0, pltpu.roll(u, 1, 1)
        )
        turned = pltpu.roll(u, NY, 1)
        above = jnp.where(z_last, 0.0, pltpu.roll(turned, chunks - 1, 0))
        below = jnp.where(z_first, 0.0, pltpu.roll(turned, 1, 0))
        return grad_y, jnp.where(low, turned - below, above - turned)

    def correlate_yz(f, carry):
        for r in range(2):
            grads = [
                differences(rows[r, f, i]) for i in range(4)
            ]
            (fr_y, fr_z), (fi_y, fi_z), (ar_y, ar_z), (ai_y, ai_z) = grads
            yz_corr[r, 0, f] = fr_y * ar_y - fi_y * ai_y + (fr_z * ar_z - fi_z * ai_z)
            yz_corr[r, 1, f] = fr_y * ai_y + fi_y * ar_y + (fr_z * ai_z + fi_z * ar_z)
        return carry

    lax.fori_loop(0, count, correlate_yz, 0)

    @pl.when(odd == 1)
    def _():
        pl.semaphore_wait(barrier, second_count)
        pl.semaphore_signal(second_sem, inc=1, device_id=(s, h, first_core), device_id_type=MESH)

    @pl.when(odd == 0)
    def _():
        pl.semaphore_wait(second_sem, 1)

    to_partner(0).wait_recv()
    pair = pl.ds(pl.multiple_of(16 * s, 16), 16)
    for step in steps:
        pltpu.make_async_remote_copy(
            src_ref=params.at[pair],
            dst_ref=params.at[pair],
            send_sem=gather_sem.at[0],
            recv_sem=gather_sem.at[1 + s // places],
            device_id=(along(step), h, b),
            device_id_type=MESH,
        ).start()
    others = pl.ds(0, 16 * (n_src - 1))

    def gathered(g, count_of):
        there = pl.ds(0, 16 * count_of)
        return pltpu.make_async_remote_copy(
            src_ref=partial.at[there],
            dst_ref=params.at[there],
            send_sem=gather_sem.at[0],
            recv_sem=gather_sem.at[1 + g],
            device_id=(along(1), h, b),
            device_id_type=MESH,
        )

    weight = jnp.float32(0.0)
    for g in range(GROUPS):
        weight = weight + jnp.where(source_group[0] == g, group_weight[g], 0.0)
    scale = weight * (0.25 / math.sqrt(n_src * 2 * count))

    for f in range(count):
        index = frequency_index[h * count + f].astype(f32)
        value = math.log(2.0 * math.pi) + math.log(10.0) * (-1.0 + (4.0 / (2 * count - 1)) * index)
        log_omega[f] = jnp.full((size, LANES), value, f32)

    for g in range(groups):
        inside_group = s // places == g
        if places > 1:
            where_there(inside_group, lambda g=g: gathered(g, places - 1).wait_recv())
        where_there(jnp.logical_not(inside_group), lambda g=g: gathered(g, places).wait_recv())
        for r in range(2):
            sigma, chg, tau, expo = (
                params[pl.ds(8 * size * g + 2 * p + r, size, stride=8), :] for p in range(4)
            )
            sigma = jnp.exp(sigma) * scale
            angle = expo * (0.5 * math.pi)
            cosine, sine = jnp.cos(angle), jnp.sin(angle)
            rest = 1.0 - chg
            q_scale = sigma * chg
            log_product = log_omega[...] + tau
            amplitude = jnp.exp(expo * log_product)
            z_r, z_i = amplitude * cosine, amplitude * sine
            d_r, d_i = 1.0 + rest * z_r, rest * z_i
            inverse = 1.0 / (d_r * d_r + d_i * d_i)
            r_r, r_i = d_r * inverse, -d_i * inverse
            s_r, s_i = (1.0 + z_r) * r_r - z_i * r_i, (1.0 + z_r) * r_i + z_i * r_r
            t_r, t_i = z_r * r_r - z_i * r_i, z_r * r_i + z_i * r_r
            s_r, s_i = sigma * s_r, sigma * s_i
            q_r, q_i = q_scale * (t_r * r_r - t_i * r_i), q_scale * (t_r * r_i + t_i * r_r)
            parts = (
                (s_r, s_i),
                (s_r * t_r - s_i * t_i, s_r * t_i + s_i * t_r),
                (expo * q_r, expo * q_i),
                (
                    q_r * log_product - (0.5 * math.pi) * q_i,
                    (0.5 * math.pi) * q_r + q_i * log_product,
                ),
            )
            for p, (part_r, part_i) in enumerate(parts):
                derivs[r, 2 * p] = part_r
                derivs[r, 2 * p + 1] = part_i

        where_there(has_prev, lambda g=g: up(g).wait_recv())
        where_there(has_next, lambda g=g: down(g).wait_recv())
        for r in range(2):
            ahead = rows.at[1] if r == 0 else from_next
            behind = from_prev if r == 0 else rows.at[0]
            f_r, f_i, a_r, a_i = (
                ahead[:, i, part(g), :] - behind[:, i, part(g), :] for i in range(4)
            )
            c_r = f_r * a_r - f_i * a_i + yz_corr[r, 0, :, part(g), :]
            c_i = f_r * a_i + f_i * a_r + yz_corr[r, 1, :, part(g), :]
            for p in range(4):
                gradient = jnp.sum(derivs[r, 2 * p] * c_r - derivs[r, 2 * p + 1] * c_i, axis=0)
                partial[pl.ds(8 * size * g + 2 * p + r, size, stride=8), :] = gradient

        for i in range(places):
            to = places * g + lax.rem(s + i, places)

            @pl.when(s != to)
            def _():
                pltpu.make_async_remote_copy(
                    src_ref=partial.at[pl.ds(pl.multiple_of(16 * to, 16), 16)],
                    dst_ref=arrived.at[pair],
                    send_sem=scatter_sem.at[0],
                    recv_sem=scatter_sem.at[1],
                    device_id=(to, h, b),
                    device_id_type=MESH,
                ).start()

    to_partner(1).wait_recv()
    mask = masks[...]
    scattered = pltpu.make_async_remote_copy(
        src_ref=partial.at[others],
        dst_ref=arrived.at[others],
        send_sem=scatter_sem.at[0],
        recv_sem=scatter_sem.at[1],
        device_id=(along(1), h, b),
        device_id_type=MESH,
    )
    scattered.wait_recv()
    arrived[pair, :] = partial[pair, :]
    tiles = [arrived[pl.ds(16 * i, 16), :] for i in range(n_src)]
    while len(tiles) > 1:
        tiles = [
            tiles[i] + tiles[i + 1] if i + 1 < len(tiles) else tiles[i]
            for i in range(0, len(tiles), 2)
        ]
    window[in_window(1, h, 8 - 8 * h, 16), :] = tiles[0] * mask

    def to_near(entry):
        there, part, device, (start, length), slot, kind = sends[entry]
        return pltpu.make_async_remote_copy(
            src_ref=window.at[in_window(1, h, 8 - 8 * h + part, length)],
            dst_ref=window.at[in_window(slot, h, start, length)],
            send_sem=near_send.at[entry],
            recv_sem=near_recv.at[4 * slot + 2 * h + kind],
            device_id=device,
            device_id_type=MESH,
        )

    def from_near(entry):
        there, device, (start, length), slot, other, kind = receives[entry]
        part = window.at[in_window(slot, other, start, length)]
        return pltpu.make_async_remote_copy(
            src_ref=part,
            dst_ref=part,
            send_sem=near_send.at[0],
            recv_sem=near_recv.at[4 * slot + 2 * other + kind],
            device_id=device,
            device_id_type=MESH,
        )

    for entry in range(len(sends)):
        where_there(sends[entry][0], lambda entry=entry: to_near(entry).start())

    tile_lane = lax.broadcasted_iota(jnp.int32, (8, LANES), 1)
    tile_line = lax.broadcasted_iota(jnp.int32, (8, LANES), 0)
    tile_low = tile_lane < NY
    tile_y = jnp.bitwise_and(tile_lane, NY - 1)
    top, bottom = tile_y == NY - 1, tile_y == 0
    first_row = jnp.bitwise_and(tile_line, 1) == 0
    smooth = []
    for d in range(3):
        w = jnp.full((8, LANES), prior_weight[0, d], f32)
        for p in range(1, 4):
            w = jnp.where(tile_line >= 2 * p, prior_weight[p, d], w)
        smooth.append(w)

    def one_pass(mid, prev, after, lower, upper):
        x_sum = jnp.where(first_row, pltpu.roll(mid, 7, 0), pltpu.roll(after, 1, 0)) + jnp.where(
            first_row, pltpu.roll(prev, 7, 0), pltpu.roll(mid, 1, 0)
        )
        y_sum = jnp.where(top, 0.0, pltpu.roll(mid, LANES - 1, 1)) + jnp.where(
            bottom, 0.0, pltpu.roll(mid, 1, 1)
        )
        turned = pltpu.roll(mid, NY, 1)
        z_sum = jnp.where(tile_low, turned, pltpu.roll(upper, NY, 1)) + jnp.where(
            tile_low, pltpu.roll(lower, NY, 1), turned
        )
        twice = 2.0 * mid
        return (
            mid
            + smooth[0] * (x_sum - twice)
            + smooth[1] * (y_sum - twice)
            + smooth[2] * (z_sum - twice)
        )

    for entry in range(len(receives)):
        where_there(receives[entry][0], lambda entry=entry: from_near(entry).wait_recv())

    def tile(db, dk):
        return sum(window[in_window(db + 1, other, 8 * (dk + 1), 8), :] for other in range(2))

    empty = jnp.zeros((8, LANES), f32)

    def inside(there, value):
        return jnp.where(there, value, 0.0)

    middle = tile(0, 0)
    mid = one_pass(middle, tile(-1, 0), tile(1, 0), tile(0, -1), tile(0, 1))
    prev = one_pass(tile(-1, 0), empty, middle, tile(-1, -1), tile(-1, 1))
    after = one_pass(tile(1, 0), middle, empty, tile(1, -1), tile(1, 1))
    lower = one_pass(tile(0, -1), tile(-1, -1), tile(1, -1), empty, middle)
    upper = one_pass(tile(0, 1), tile(-1, 1), tile(1, 1), middle, empty)
    out[...] = one_pass(
        mid,
        inside(has_prev, prev),
        inside(has_next, after),
        inside(k > 0, lower),
        inside(k < chunks - 1, upper),
    )

    for g in range(groups):
        where_there(has_next, lambda g=g: up(g).wait_send())
        where_there(has_prev, lambda g=g: down(g).wait_send())
    to_partner(0).wait_send()
    to_partner(1).wait_send()
    gathered(0, n_src - 1).wait_send()
    scattered.wait_send()
    for entry in range(len(sends)):
        where_there(sends[entry][0], lambda entry=entry: to_near(entry).wait_send())


def solution(mesh):
    n_src, n_space = mesh.shape["src"], mesh.shape["space"]
    chunks = 2 * n_src

    def local(
        forward,
        adjoint,
        source_group,
        group_weight,
        frequency_index,
        log_sigma,
        charge,
        log_tau,
        exponent,
        active,
        prior_weight,
    ):
        count = forward.shape[1]
        size = min(8, chunks)
        groups = chunks // size

        def keep(x):
            return pltpu.with_memory_space_constraint(x, pltpu.HBM)

        def lines(field):
            split = field.reshape(count, 2, 2, chunks, LANES)
            return split.transpose(0, 1, 3, 2, 4).reshape(count, 4 * chunks, LANES)

        hbm = pl.BlockSpec(memory_space=pl.ANY)
        vmem = pl.BlockSpec(memory_space=pltpu.VMEM)
        smem = pl.BlockSpec(memory_space=pltpu.SMEM)
        f32 = jnp.float32
        result = pl.pallas_call(
            functools.partial(kernel, (n_src, n_space, count)),
            out_shape=jax.ShapeDtypeStruct((8, LANES), f32),
            in_specs=[hbm] * 7 + [smem] * 4,
            out_specs=vmem,
            scratch_shapes=[
                pltpu.VMEM((4, 2, LANES), f32),
                pltpu.VMEM((2, LANES), jnp.int32),
                pltpu.VMEM((2, count, 4 * chunks, LANES), f32),
                pltpu.VMEM((2, count, 4, chunks, LANES), f32),
                pltpu.VMEM((count, 4, chunks, LANES), f32),
                pltpu.VMEM((count, 4, chunks, LANES), f32),
                pltpu.VMEM((8 * chunks, LANES), f32),
                pltpu.VMEM((16, LANES), f32),
                pltpu.VMEM((8 * chunks, LANES), f32),
                pltpu.VMEM((8 * chunks, LANES), f32),
                pltpu.VMEM((6 * 24, LANES), f32),
                pltpu.VMEM((2, 8, count, size, LANES), f32),
                pltpu.VMEM((2, 2, count, chunks, LANES), f32),
                pltpu.VMEM((count, size, LANES), f32),
                pltpu.SemaphoreType.DMA((2,)),
                pltpu.SemaphoreType.DMA((5,)),
                pltpu.SemaphoreType.DMA((2, groups)),
                pltpu.SemaphoreType.DMA((2, groups)),
                pltpu.SemaphoreType.DMA((2,)),
                pltpu.SemaphoreType.DMA((2,)),
                pltpu.SemaphoreType.DMA((1 + groups,)),
                pltpu.SemaphoreType.DMA((2,)),
                pltpu.SemaphoreType.DMA((11,)),
                pltpu.SemaphoreType.DMA((12,)),
                pltpu.SemaphoreType.REGULAR,
                pltpu.SemaphoreType.REGULAR,
            ],
            compiler_params=pltpu.CompilerParams(
                collective_id=0, has_side_effects=True, vmem_limit_bytes=32 * 1024 * 1024
            ),
        )(
            *map(keep, (lines(forward), lines(adjoint), log_sigma, charge, log_tau, exponent, active)),
            source_group,
            *map(keep, (group_weight, frequency_index, prior_weight)),
        )
        return result.reshape(4, 2, LANES)

    placed = (
        P("src", "freq", None, "space", None),
        P("src", "freq", None, "space", None),
        P("src"),
        P(),
        P(),
        P("space", ("src", "freq")),
        P("space", ("src", "freq")),
        P("space", ("src", "freq")),
        P("space", ("src", "freq")),
        P("space", ("src", "freq")),
        P(),
    )
    return jax.shard_map(
        local,
        mesh=mesh,
        in_specs=placed,
        out_specs=P(None, "space", ("src", "freq")),
        check_vma=False,
    )
```

```python
import functools
import math

import jax
import jax.numpy as jnp
from jax import lax
from jax.experimental import pallas as pl
from jax.experimental.pallas import tpu as pltpu
from jax.sharding import PartitionSpec as P

MESH = pl.DeviceIdType.MESH
GROUPS = 3
NY = 64
LANES = 128


def kernel(
    sizes,
    forward,
    adjoint,
    log_sigma,
    charge,
    log_tau,
    exponent,
    active_in,
    source_group,
    group_weight_in,
    frequency_index_in,
    prior_weight_in,
    out,
    cell_params,
    active,
    group_weight,
    frequency_index,
    prior_weight,
    own,
    rows,
    from_prev,
    from_next,
    params,
    masks,
    partial,
    arrived,
    window,
    derivs,
    yz_corr,
    log_omega,
    load_sem,
    small_sem,
    halo_send,
    halo_recv,
    pair_send,
    pair_recv,
    gather_sem,
    scatter_sem,
    near_send,
    near_recv,
    first_sem,
    second_sem,
):
    n_src, n_space, count = sizes
    chunks = 2 * n_src
    half = 2 * chunks
    size = min(8, chunks)
    groups = chunks // size
    places = size // 2
    s, h, b = lax.axis_index("src"), lax.axis_index("freq"), lax.axis_index("space")
    k = 2 * s + h
    f32 = jnp.float32
    steps = sorted(range(1, n_src), key=lambda step: -min(step, n_src - step))

    def along(step):
        return lax.rem(s + step, n_src)

    loads = [
        pltpu.make_async_copy(field, own.at[i], load_sem.at[i])
        for i, field in enumerate((forward, adjoint))
    ]
    small = [
        pltpu.make_async_copy(source, target, small_sem.at[i])
        for i, (source, target) in enumerate(
            (
                (log_sigma, cell_params.at[0]),
                (charge, cell_params.at[1]),
                (log_tau, cell_params.at[2]),
                (exponent, cell_params.at[3]),
                (active_in, active),
                (group_weight_in, group_weight),
                (frequency_index_in, frequency_index),
                (prior_weight_in, prior_weight),
            )
        )
    ]
    has_prev, has_next = b > 0, b < n_space - 1
    beside = {-1: has_prev, 0: None, 1: has_next}

    def both(first, second):
        if first is None or second is None:
            return second if first is None else first
        return jnp.logical_and(first, second)

    def in_window(slot, share, start, length):
        return pl.ds(pl.multiple_of(48 * slot + 24 * share + start, 8), length)

    def where_there(there, act):
        if there is None:
            act()
        else:
            pl.when(there)(act)

    side, away = s - 1 + 2 * h, s + 1 - 2 * h
    has_side = jnp.logical_and(side >= 0, side < n_src)
    has_away = jnp.logical_and(away >= 0, away < n_src)
    sends = []
    for db in (-1, 1, 0):
        there = both(has_side, beside[db])
        sends.append((there, 8 * h, (side, 1 - h, b + db), (16 - 16 * h, 8), 1 - db, 1))
        sends.append((beside[db], 0, (s, 1 - h, b + db), (8 * h, 16), 1 - db, 0))
    for db in (-1, 1, 0):
        there = both(has_away, beside[db])
        sends.append((there, 8 - 8 * h, (away, h, b + db), (16 * h, 8), 1 - db, 1))
        if db != 0:
            sends.append((beside[db], 0, (s, h, b + db), (8 - 8 * h, 16), 1 - db, 0))
    receives = []
    for db in (-1, 0, 1):
        if db != 0:
            receives.append((beside[db], (s, h, b + db), (8 - 8 * h, 16), 1 + db, h, 0))
        receives.append((beside[db], (s, 1 - h, b + db), (8 - 8 * h, 16), 1 + db, 1 - h, 0))
        for other in (h, 1 - h):
            there = both(has_side, beside[db])
            receives.append((there, (side, other, b + db), (16 * h, 8), 1 + db, other, 1))

    odd = lax.rem(b, 2)
    first_core, second_core = b - odd, b - odd + 1
    next_chip = first_core - 2 + 4 * odd
    has_chip = jnp.logical_and(next_chip >= 0, next_chip < n_space)
    barrier = pltpu.get_barrier_semaphore()

    def greet(*device):
        pl.semaphore_signal(barrier, inc=1, device_id=device, device_id_type=MESH)

    for step in steps:
        greet(along(step), h, second_core)
    where_there(odd == 1, functools.partial(greet, s, h, first_core))
    where_there(has_chip, functools.partial(greet, s, h, next_chip))
    greet(s, 1 - h, first_core)
    for load in loads + small:
        load.start()
    where_there(both(has_side, has_chip), functools.partial(greet, side, 1 - h, next_chip + 1))
    where_there(has_side, functools.partial(greet, side, 1 - h, second_core))
    where_there(has_chip, functools.partial(greet, s, 1 - h, next_chip + 1))
    where_there(both(has_side, has_chip), functools.partial(greet, side, h, next_chip + 1))

    chips = (first_core > 0).astype(jnp.int32) + (second_core < n_space - 1).astype(jnp.int32)
    to_side, to_away = has_side.astype(jnp.int32), has_away.astype(jnp.int32)
    first_count = 3 + chips
    second_count = 2 * (n_src - 1) + chips * (1 + to_side + to_away) + 2 * to_side

    mine = pl.ds(pl.multiple_of(8 * k, 8), 8)
    my_half = pl.ds(pl.multiple_of(8 * h, 8), 8)
    for load in small:
        load.wait()
    params[mine, :] = jnp.concatenate([cell_params[p] for p in range(4)], axis=0)
    masks[my_half, :] = jnp.concatenate([active[...].astype(f32)] * 4, axis=0)

    for load in loads:
        load.wait()

    def split_rows(f, carry):
        for i in range(2):
            for r in range(2):
                for c in range(2):
                    first = half * c + r
                    rows[r, f, 2 * i + c] = own[i, f, pl.ds(first, chunks, stride=2), :]
        return carry

    lax.fori_loop(0, count, split_rows, 0)

    @pl.when(jnp.logical_not(has_prev))
    def _():
        from_prev[...] = jnp.zeros_like(from_prev)
        window[pl.ds(0, 48), :] = jnp.zeros((48, LANES), f32)

    @pl.when(jnp.logical_not(has_next))
    def _():
        from_next[...] = jnp.zeros_like(from_next)
        window[pl.ds(96, 48), :] = jnp.zeros((48, LANES), f32)

    @pl.when(jnp.logical_not(has_side))
    def _():
        for db in range(3):
            for other in range(2):
                window[in_window(db, other, 16 * h, 8), :] = jnp.zeros((8, LANES), f32)

    @pl.when(odd == 0)
    def _():
        pl.semaphore_wait(barrier, first_count)
        pl.semaphore_signal(first_sem, inc=1, device_id=(s, h, second_core), device_id_type=MESH)

    @pl.when(odd == 1)
    def _():
        pl.semaphore_wait(first_sem, 1)

    def to_partner(i):
        ref, part = ((params, mine), (masks, my_half))[i]
        return pltpu.make_async_remote_copy(
            src_ref=ref.at[part],
            dst_ref=ref.at[part],
            send_sem=pair_send.at[i],
            recv_sem=pair_recv.at[i],
            device_id=(s, 1 - h, b),
            device_id_type=MESH,
        )

    to_partner(0).start()

    def part(g):
        return pl.ds(size * g, size)

    def up(g):
        return pltpu.make_async_remote_copy(
            src_ref=rows.at[1, :, :, part(g), :],
            dst_ref=from_prev.at[:, :, part(g), :],
            send_sem=halo_send.at[0, g],
            recv_sem=halo_recv.at[0, g],
            device_id=(s, h, b + 1),
            device_id_type=MESH,
        )

    def down(g):
        return pltpu.make_async_remote_copy(
            src_ref=rows.at[0, :, :, part(g), :],
            dst_ref=from_next.at[:, :, part(g), :],
            send_sem=halo_send.at[1, g],
            recv_sem=halo_recv.at[1, g],
            device_id=(s, h, b - 1),
            device_id_type=MESH,
        )

    for g in range(groups):
        where_there(has_next, lambda g=g: up(g).start())
        where_there(has_prev, lambda g=g: down(g).start())
    to_partner(1).start()

    lane = lax.broadcasted_iota(jnp.int32, (chunks, LANES), 1)
    line = lax.broadcasted_iota(jnp.int32, (chunks, LANES), 0)
    low = lane < NY
    y_pos = jnp.bitwise_and(lane, NY - 1)
    y_last, y_first = y_pos == NY - 1, y_pos == 0
    z_last, z_first = line == chunks - 1, line == 0

    def differences(u):
        grad_y = jnp.where(y_last, 0.0, pltpu.roll(u, LANES - 1, 1)) - jnp.where(
            y_first, 0.0, pltpu.roll(u, 1, 1)
        )
        turned = pltpu.roll(u, NY, 1)
        above = jnp.where(z_last, 0.0, pltpu.roll(turned, chunks - 1, 0))
        below = jnp.where(z_first, 0.0, pltpu.roll(turned, 1, 0))
        return grad_y, jnp.where(low, turned - below, above - turned)

    def correlate_yz(f, carry):
        for r in range(2):
            grads = [
                differences(rows[r, f, i]) for i in range(4)
            ]
            (fr_y, fr_z), (fi_y, fi_z), (ar_y, ar_z), (ai_y, ai_z) = grads
            yz_corr[r, 0, f] = fr_y * ar_y - fi_y * ai_y + (fr_z * ar_z - fi_z * ai_z)
            yz_corr[r, 1, f] = fr_y * ai_y + fi_y * ar_y + (fr_z * ai_z + fi_z * ar_z)
        return carry

    lax.fori_loop(0, count, correlate_yz, 0)

    @pl.when(odd == 1)
    def _():
        pl.semaphore_wait(barrier, second_count)
        pl.semaphore_signal(second_sem, inc=1, device_id=(s, h, first_core), device_id_type=MESH)

    @pl.when(odd == 0)
    def _():
        pl.semaphore_wait(second_sem, 1)

    to_partner(0).wait_recv()
    pair = pl.ds(pl.multiple_of(16 * s, 16), 16)
    for step in steps:
        pltpu.make_async_remote_copy(
            src_ref=params.at[pair],
            dst_ref=params.at[pair],
            send_sem=gather_sem.at[0],
            recv_sem=gather_sem.at[1 + s // places],
            device_id=(along(step), h, b),
            device_id_type=MESH,
        ).start()
    others = pl.ds(0, 16 * (n_src - 1))

    def gathered(g, count_of):
        there = pl.ds(0, 16 * count_of)
        return pltpu.make_async_remote_copy(
            src_ref=partial.at[there],
            dst_ref=params.at[there],
            send_sem=gather_sem.at[0],
            recv_sem=gather_sem.at[1 + g],
            device_id=(along(1), h, b),
            device_id_type=MESH,
        )

    weight = jnp.float32(0.0)
    for g in range(GROUPS):
        weight = weight + jnp.where(source_group[0] == g, group_weight[g], 0.0)
    scale = weight * (0.25 / math.sqrt(n_src * 2 * count))

    for f in range(count):
        index = frequency_index[h * count + f].astype(f32)
        value = math.log(2.0 * math.pi) + math.log(10.0) * (-1.0 + (4.0 / (2 * count - 1)) * index)
        log_omega[f] = jnp.full((size, LANES), value, f32)

    for g in range(groups):
        inside_group = s // places == g
        if places > 1:
            where_there(inside_group, lambda g=g: gathered(g, places - 1).wait_recv())
        where_there(jnp.logical_not(inside_group), lambda g=g: gathered(g, places).wait_recv())
        for r in range(2):
            sigma, chg, tau, expo = (
                params[pl.ds(8 * size * g + 2 * p + r, size, stride=8), :] for p in range(4)
            )
            sigma = jnp.exp(sigma) * scale
            angle = expo * (0.5 * math.pi)
            cosine, sine = jnp.cos(angle), jnp.sin(angle)
            rest = 1.0 - chg
            q_scale = sigma * chg
            log_product = log_omega[...] + tau
            amplitude = jnp.exp(expo * log_product)
            z_r, z_i = amplitude * cosine, amplitude * sine
            d_r, d_i = 1.0 + rest * z_r, rest * z_i
            inverse = 1.0 / (d_r * d_r + d_i * d_i)
            r_r, r_i = d_r * inverse, -d_i * inverse
            s_r, s_i = (1.0 + z_r) * r_r - z_i * r_i, (1.0 + z_r) * r_i + z_i * r_r
            t_r, t_i = z_r * r_r - z_i * r_i, z_r * r_i + z_i * r_r
            s_r, s_i = sigma * s_r, sigma * s_i
            q_r, q_i = q_scale * (t_r * r_r - t_i * r_i), q_scale * (t_r * r_i + t_i * r_r)
            parts = (
                (s_r, s_i),
                (s_r * t_r - s_i * t_i, s_r * t_i + s_i * t_r),
                (expo * q_r, expo * q_i),
                (
                    q_r * log_product - (0.5 * math.pi) * q_i,
                    (0.5 * math.pi) * q_r + q_i * log_product,
                ),
            )
            for p, (part_r, part_i) in enumerate(parts):
                derivs[r, 2 * p] = part_r
                derivs[r, 2 * p + 1] = part_i

        where_there(has_prev, lambda g=g: up(g).wait_recv())
        where_there(has_next, lambda g=g: down(g).wait_recv())
        for r in range(2):
            ahead = rows.at[1] if r == 0 else from_next
            behind = from_prev if r == 0 else rows.at[0]
            f_r, f_i, a_r, a_i = (
                ahead[:, i, part(g), :] - behind[:, i, part(g), :] for i in range(4)
            )
            c_r = f_r * a_r - f_i * a_i + yz_corr[r, 0, :, part(g), :]
            c_i = f_r * a_i + f_i * a_r + yz_corr[r, 1, :, part(g), :]
            for p in range(4):
                gradient = jnp.sum(derivs[r, 2 * p] * c_r - derivs[r, 2 * p + 1] * c_i, axis=0)
                partial[pl.ds(8 * size * g + 2 * p + r, size, stride=8), :] = gradient

        for i in range(places):
            to = places * g + lax.rem(s + i, places)

            @pl.when(s != to)
            def _():
                pltpu.make_async_remote_copy(
                    src_ref=partial.at[pl.ds(pl.multiple_of(16 * to, 16), 16)],
                    dst_ref=arrived.at[pair],
                    send_sem=scatter_sem.at[0],
                    recv_sem=scatter_sem.at[1],
                    device_id=(to, h, b),
                    device_id_type=MESH,
                ).start()

    to_partner(1).wait_recv()
    mask = masks[...]
    scattered = pltpu.make_async_remote_copy(
        src_ref=partial.at[others],
        dst_ref=arrived.at[others],
        send_sem=scatter_sem.at[0],
        recv_sem=scatter_sem.at[1],
        device_id=(along(1), h, b),
        device_id_type=MESH,
    )
    scattered.wait_recv()
    arrived[pair, :] = partial[pair, :]
    tiles = [arrived[pl.ds(16 * i, 16), :] for i in range(n_src)]
    while len(tiles) > 1:
        tiles = [
            tiles[i] + tiles[i + 1] if i + 1 < len(tiles) else tiles[i]
            for i in range(0, len(tiles), 2)
        ]
    window[in_window(1, h, 8 - 8 * h, 16), :] = tiles[0] * mask

    def to_near(entry):
        there, part, device, (start, length), slot, kind = sends[entry]
        return pltpu.make_async_remote_copy(
            src_ref=window.at[in_window(1, h, 8 - 8 * h + part, length)],
            dst_ref=window.at[in_window(slot, h, start, length)],
            send_sem=near_send.at[entry],
            recv_sem=near_recv.at[4 * slot + 2 * h + kind],
            device_id=device,
            device_id_type=MESH,
        )

    def from_near(entry):
        there, device, (start, length), slot, other, kind = receives[entry]
        part = window.at[in_window(slot, other, start, length)]
        return pltpu.make_async_remote_copy(
            src_ref=part,
            dst_ref=part,
            send_sem=near_send.at[0],
            recv_sem=near_recv.at[4 * slot + 2 * other + kind],
            device_id=device,
            device_id_type=MESH,
        )

    for entry in range(len(sends)):
        where_there(sends[entry][0], lambda entry=entry: to_near(entry).start())

    tile_lane = lax.broadcasted_iota(jnp.int32, (8, LANES), 1)
    tile_line = lax.broadcasted_iota(jnp.int32, (8, LANES), 0)
    tile_low = tile_lane < NY
    tile_y = jnp.bitwise_and(tile_lane, NY - 1)
    top, bottom = tile_y == NY - 1, tile_y == 0
    first_row = jnp.bitwise_and(tile_line, 1) == 0
    smooth = []
    for d in range(3):
        w = jnp.full((8, LANES), prior_weight[0, d], f32)
        for p in range(1, 4):
            w = jnp.where(tile_line >= 2 * p, prior_weight[p, d], w)
        smooth.append(w)

    def one_pass(mid, prev, after, lower, upper):
        x_sum = jnp.where(first_row, pltpu.roll(mid, 7, 0), pltpu.roll(after, 1, 0)) + jnp.where(
            first_row, pltpu.roll(prev, 7, 0), pltpu.roll(mid, 1, 0)
        )
        y_sum = jnp.where(top, 0.0, pltpu.roll(mid, LANES - 1, 1)) + jnp.where(
            bottom, 0.0, pltpu.roll(mid, 1, 1)
        )
        turned = pltpu.roll(mid, NY, 1)
        z_sum = jnp.where(tile_low, turned, pltpu.roll(upper, NY, 1)) + jnp.where(
            tile_low, pltpu.roll(lower, NY, 1), turned
        )
        twice = 2.0 * mid
        return (
            mid
            + smooth[0] * (x_sum - twice)
            + smooth[1] * (y_sum - twice)
            + smooth[2] * (z_sum - twice)
        )

    for g in range(groups):
        where_there(has_next, lambda g=g: up(g).wait_send())
        where_there(has_prev, lambda g=g: down(g).wait_send())
    to_partner(0).wait_send()
    to_partner(1).wait_send()
    gathered(0, n_src - 1).wait_send()
    scattered.wait_send()

    for entry in range(len(receives)):
        where_there(receives[entry][0], lambda entry=entry: from_near(entry).wait_recv())

    def tile(db, dk):
        return sum(window[in_window(db + 1, other, 8 * (dk + 1), 8), :] for other in range(2))

    empty = jnp.zeros((8, LANES), f32)

    def inside(there, value):
        return jnp.where(there, value, 0.0)

    middle = tile(0, 0)
    mid = one_pass(middle, tile(-1, 0), tile(1, 0), tile(0, -1), tile(0, 1))
    prev = one_pass(tile(-1, 0), empty, middle, tile(-1, -1), tile(-1, 1))
    after = one_pass(tile(1, 0), middle, empty, tile(1, -1), tile(1, 1))
    lower = one_pass(tile(0, -1), tile(-1, -1), tile(1, -1), empty, middle)
    upper = one_pass(tile(0, 1), tile(-1, 1), tile(1, 1), middle, empty)
    out[...] = one_pass(
        mid,
        inside(has_prev, prev),
        inside(has_next, after),
        inside(k > 0, lower),
        inside(k < chunks - 1, upper),
    )

    for entry in range(len(sends)):
        where_there(sends[entry][0], lambda entry=entry: to_near(entry).wait_send())


def solution(mesh):
    n_src, n_space = mesh.shape["src"], mesh.shape["space"]
    chunks = 2 * n_src

    def local(
        forward,
        adjoint,
        source_group,
        group_weight,
        frequency_index,
        log_sigma,
        charge,
        log_tau,
        exponent,
        active,
        prior_weight,
    ):
        count = forward.shape[1]
        size = min(8, chunks)
        groups = chunks // size

        def keep(x):
            return pltpu.with_memory_space_constraint(x, pltpu.HBM)

        def lines(field):
            split = field.reshape(count, 2, 2, chunks, LANES)
            return split.transpose(0, 1, 3, 2, 4).reshape(count, 4 * chunks, LANES)

        hbm = pl.BlockSpec(memory_space=pl.ANY)
        vmem = pl.BlockSpec(memory_space=pltpu.VMEM)
        smem = pl.BlockSpec(memory_space=pltpu.SMEM)
        f32 = jnp.float32
        result = pl.pallas_call(
            functools.partial(kernel, (n_src, n_space, count)),
            out_shape=jax.ShapeDtypeStruct((8, LANES), f32),
            in_specs=[hbm] * 7 + [smem] + [hbm] * 3,
            out_specs=vmem,
            scratch_shapes=[
                pltpu.VMEM((4, 2, LANES), f32),
                pltpu.VMEM((2, LANES), jnp.int32),
                pltpu.SMEM(group_weight.shape, f32),
                pltpu.SMEM(frequency_index.shape, jnp.int32),
                pltpu.SMEM(prior_weight.shape, f32),
                pltpu.VMEM((2, count, 4 * chunks, LANES), f32),
                pltpu.VMEM((2, count, 4, chunks, LANES), f32),
                pltpu.VMEM((count, 4, chunks, LANES), f32),
                pltpu.VMEM((count, 4, chunks, LANES), f32),
                pltpu.VMEM((8 * chunks, LANES), f32),
                pltpu.VMEM((16, LANES), f32),
                pltpu.VMEM((8 * chunks, LANES), f32),
                pltpu.VMEM((8 * chunks, LANES), f32),
                pltpu.VMEM((6 * 24, LANES), f32),
                pltpu.VMEM((2, 8, count, size, LANES), f32),
                pltpu.VMEM((2, 2, count, chunks, LANES), f32),
                pltpu.VMEM((count, size, LANES), f32),
                pltpu.SemaphoreType.DMA((2,)),
                pltpu.SemaphoreType.DMA((8,)),
                pltpu.SemaphoreType.DMA((2, groups)),
                pltpu.SemaphoreType.DMA((2, groups)),
                pltpu.SemaphoreType.DMA((2,)),
                pltpu.SemaphoreType.DMA((2,)),
                pltpu.SemaphoreType.DMA((1 + groups,)),
                pltpu.SemaphoreType.DMA((2,)),
                pltpu.SemaphoreType.DMA((11,)),
                pltpu.SemaphoreType.DMA((12,)),
                pltpu.SemaphoreType.REGULAR,
                pltpu.SemaphoreType.REGULAR,
            ],
            compiler_params=pltpu.CompilerParams(
                collective_id=0, has_side_effects=True, vmem_limit_bytes=32 * 1024 * 1024
            ),
        )(
            *map(keep, (lines(forward), lines(adjoint), log_sigma, charge, log_tau, exponent, active)),
            source_group,
            *map(keep, (group_weight, frequency_index, prior_weight)),
        )
        return result.reshape(4, 2, LANES)

    placed = (
        P("src", "freq", None, "space", None),
        P("src", "freq", None, "space", None),
        P("src"),
        P(),
        P(),
        P("space", ("src", "freq")),
        P("space", ("src", "freq")),
        P("space", ("src", "freq")),
        P("space", ("src", "freq")),
        P("space", ("src", "freq")),
        P(),
    )
    return jax.shard_map(
        local,
        mesh=mesh,
        in_specs=placed,
        out_specs=P(None, "space", ("src", "freq")),
        check_vma=False,
    )
```

```python
import functools
import math

import jax
import jax.numpy as jnp
from jax import lax
from jax.experimental import pallas as pl
from jax.experimental.pallas import tpu as pltpu
from jax.sharding import PartitionSpec as P

MESH = pl.DeviceIdType.MESH
GROUPS = 3
NY = 64
LANES = 128


def kernel(
    sizes,
    forward,
    adjoint,
    log_sigma,
    charge,
    log_tau,
    exponent,
    active_in,
    source_group,
    group_weight_in,
    frequency_index_in,
    prior_weight_in,
    out,
    cell_params,
    active,
    group_weight,
    frequency_index,
    prior_weight,
    own,
    rows,
    from_prev,
    from_next,
    params,
    masks,
    partial,
    arrived,
    window,
    derivs,
    yz_corr,
    log_omega,
    load_sem,
    small_sem,
    halo_send,
    halo_recv,
    pair_send,
    pair_recv,
    gather_sem,
    scatter_sem,
    near_send,
    near_recv,
    first_sem,
    second_sem,
):
    n_src, n_space, count = sizes
    chunks = 2 * n_src
    half = 2 * chunks
    size = min(8, chunks)
    groups = chunks // size
    places = size // 2
    s, h, b = lax.axis_index("src"), lax.axis_index("freq"), lax.axis_index("space")
    k = 2 * s + h
    f32 = jnp.float32
    steps = sorted(range(1, n_src), key=lambda step: -min(step, n_src - step))

    def along(step):
        return lax.rem(s + step, n_src)

    loads = [
        pltpu.make_async_copy(field, own.at[i], load_sem.at[i])
        for i, field in enumerate((forward, adjoint))
    ]
    small = [
        pltpu.make_async_copy(source, target, small_sem.at[i])
        for i, (source, target) in enumerate(
            (
                (log_sigma, cell_params.at[0]),
                (charge, cell_params.at[1]),
                (log_tau, cell_params.at[2]),
                (exponent, cell_params.at[3]),
                (active_in, active),
                (group_weight_in, group_weight),
                (frequency_index_in, frequency_index),
                (prior_weight_in, prior_weight),
            )
        )
    ]
    has_prev, has_next = b > 0, b < n_space - 1
    beside = {-1: has_prev, 0: None, 1: has_next}

    def both(first, second):
        if first is None or second is None:
            return second if first is None else first
        return jnp.logical_and(first, second)

    def in_window(slot, share, start, length):
        return pl.ds(pl.multiple_of(48 * slot + 24 * share + start, 8), length)

    def where_there(there, act):
        if there is None:
            act()
        else:
            pl.when(there)(act)

    side, away = s - 1 + 2 * h, s + 1 - 2 * h
    has_side = jnp.logical_and(side >= 0, side < n_src)
    has_away = jnp.logical_and(away >= 0, away < n_src)
    sends = []
    for db in (-1, 1, 0):
        there = both(has_side, beside[db])
        sends.append((there, 8 * h, (side, 1 - h, b + db), (16 - 16 * h, 8), 1 - db, 1))
        sends.append((beside[db], 0, (s, 1 - h, b + db), (8 * h, 16), 1 - db, 0))
    for db in (-1, 1, 0):
        there = both(has_away, beside[db])
        sends.append((there, 8 - 8 * h, (away, h, b + db), (16 * h, 8), 1 - db, 1))
        if db != 0:
            sends.append((beside[db], 0, (s, h, b + db), (8 - 8 * h, 16), 1 - db, 0))
    receives = []
    for db in (-1, 1):
        receives.append((beside[db], (s, h, b + db), (8 - 8 * h, 16), 1 + db, h, 0))
    for other in (h, 1 - h):
        for db in (0, -1, 1):
            there = both(has_side, beside[db])
            receives.append((there, (side, other, b + db), (16 * h, 8), 1 + db, other, 1))
    for db in (-1, 1, 0):
        receives.append((beside[db], (s, 1 - h, b + db), (8 - 8 * h, 16), 1 + db, 1 - h, 0))

    odd = lax.rem(b, 2)
    first_core, second_core = b - odd, b - odd + 1
    next_chip = first_core - 2 + 4 * odd
    has_chip = jnp.logical_and(next_chip >= 0, next_chip < n_space)
    barrier = pltpu.get_barrier_semaphore()

    def greet(*device):
        pl.semaphore_signal(barrier, inc=1, device_id=device, device_id_type=MESH)

    for step in steps:
        greet(along(step), h, second_core)
    where_there(odd == 1, functools.partial(greet, s, h, first_core))
    where_there(has_chip, functools.partial(greet, s, h, next_chip))
    greet(s, 1 - h, first_core)
    for load in loads + small:
        load.start()
    where_there(both(has_side, has_chip), functools.partial(greet, side, 1 - h, next_chip + 1))
    where_there(has_side, functools.partial(greet, side, 1 - h, second_core))
    where_there(has_chip, functools.partial(greet, s, 1 - h, next_chip + 1))
    where_there(both(has_side, has_chip), functools.partial(greet, side, h, next_chip + 1))

    chips = (first_core > 0).astype(jnp.int32) + (second_core < n_space - 1).astype(jnp.int32)
    to_side, to_away = has_side.astype(jnp.int32), has_away.astype(jnp.int32)
    first_count = 3 + chips
    second_count = 2 * (n_src - 1) + chips * (1 + to_side + to_away) + 2 * to_side

    mine = pl.ds(pl.multiple_of(8 * k, 8), 8)
    my_half = pl.ds(pl.multiple_of(8 * h, 8), 8)
    for load in small:
        load.wait()
    params[mine, :] = jnp.concatenate([cell_params[p] for p in range(4)], axis=0)
    masks[my_half, :] = jnp.concatenate([active[...].astype(f32)] * 4, axis=0)

    for load in loads:
        load.wait()

    def split_rows(f, carry):
        for i in range(2):
            for r in range(2):
                for c in range(2):
                    first = half * c + r
                    rows[r, f, 2 * i + c] = own[i, f, pl.ds(first, chunks, stride=2), :]
        return carry

    lax.fori_loop(0, count, split_rows, 0)

    @pl.when(jnp.logical_not(has_prev))
    def _():
        from_prev[...] = jnp.zeros_like(from_prev)
        window[pl.ds(0, 48), :] = jnp.zeros((48, LANES), f32)

    @pl.when(jnp.logical_not(has_next))
    def _():
        from_next[...] = jnp.zeros_like(from_next)
        window[pl.ds(96, 48), :] = jnp.zeros((48, LANES), f32)

    @pl.when(jnp.logical_not(has_side))
    def _():
        for db in range(3):
            for other in range(2):
                window[in_window(db, other, 16 * h, 8), :] = jnp.zeros((8, LANES), f32)

    @pl.when(odd == 0)
    def _():
        pl.semaphore_wait(barrier, first_count)
        pl.semaphore_signal(first_sem, inc=1, device_id=(s, h, second_core), device_id_type=MESH)

    @pl.when(odd == 1)
    def _():
        pl.semaphore_wait(first_sem, 1)

    def to_partner(i):
        ref, part = ((params, mine), (masks, my_half))[i]
        return pltpu.make_async_remote_copy(
            src_ref=ref.at[part],
            dst_ref=ref.at[part],
            send_sem=pair_send.at[i],
            recv_sem=pair_recv.at[i],
            device_id=(s, 1 - h, b),
            device_id_type=MESH,
        )

    to_partner(0).start()

    def part(g):
        return pl.ds(size * g, size)

    def up(g):
        return pltpu.make_async_remote_copy(
            src_ref=rows.at[1, :, :, part(g), :],
            dst_ref=from_prev.at[:, :, part(g), :],
            send_sem=halo_send.at[0, g],
            recv_sem=halo_recv.at[0, g],
            device_id=(s, h, b + 1),
            device_id_type=MESH,
        )

    def down(g):
        return pltpu.make_async_remote_copy(
            src_ref=rows.at[0, :, :, part(g), :],
            dst_ref=from_next.at[:, :, part(g), :],
            send_sem=halo_send.at[1, g],
            recv_sem=halo_recv.at[1, g],
            device_id=(s, h, b - 1),
            device_id_type=MESH,
        )

    for g in range(groups):
        where_there(has_next, lambda g=g: up(g).start())
        where_there(has_prev, lambda g=g: down(g).start())
    to_partner(1).start()

    lane = lax.broadcasted_iota(jnp.int32, (chunks, LANES), 1)
    line = lax.broadcasted_iota(jnp.int32, (chunks, LANES), 0)
    low = lane < NY
    y_pos = jnp.bitwise_and(lane, NY - 1)
    y_last, y_first = y_pos == NY - 1, y_pos == 0
    z_last, z_first = line == chunks - 1, line == 0

    def differences(u):
        grad_y = jnp.where(y_last, 0.0, pltpu.roll(u, LANES - 1, 1)) - jnp.where(
            y_first, 0.0, pltpu.roll(u, 1, 1)
        )
        turned = pltpu.roll(u, NY, 1)
        above = jnp.where(z_last, 0.0, pltpu.roll(turned, chunks - 1, 0))
        below = jnp.where(z_first, 0.0, pltpu.roll(turned, 1, 0))
        return grad_y, jnp.where(low, turned - below, above - turned)

    def correlate_yz(f, carry):
        for r in range(2):
            grads = [
                differences(rows[r, f, i]) for i in range(4)
            ]
            (fr_y, fr_z), (fi_y, fi_z), (ar_y, ar_z), (ai_y, ai_z) = grads
            yz_corr[r, 0, f] = fr_y * ar_y - fi_y * ai_y + (fr_z * ar_z - fi_z * ai_z)
            yz_corr[r, 1, f] = fr_y * ai_y + fi_y * ar_y + (fr_z * ai_z + fi_z * ar_z)
        return carry

    lax.fori_loop(0, count, correlate_yz, 0)

    @pl.when(odd == 1)
    def _():
        pl.semaphore_wait(barrier, second_count)
        pl.semaphore_signal(second_sem, inc=1, device_id=(s, h, first_core), device_id_type=MESH)

    @pl.when(odd == 0)
    def _():
        pl.semaphore_wait(second_sem, 1)

    to_partner(0).wait_recv()
    pair = pl.ds(pl.multiple_of(16 * s, 16), 16)
    for step in steps:
        pltpu.make_async_remote_copy(
            src_ref=params.at[pair],
            dst_ref=params.at[pair],
            send_sem=gather_sem.at[0],
            recv_sem=gather_sem.at[1 + s // places],
            device_id=(along(step), h, b),
            device_id_type=MESH,
        ).start()
    others = pl.ds(0, 16 * (n_src - 1))

    def gathered(g, count_of):
        there = pl.ds(0, 16 * count_of)
        return pltpu.make_async_remote_copy(
            src_ref=partial.at[there],
            dst_ref=params.at[there],
            send_sem=gather_sem.at[0],
            recv_sem=gather_sem.at[1 + g],
            device_id=(along(1), h, b),
            device_id_type=MESH,
        )

    weight = jnp.float32(0.0)
    for g in range(GROUPS):
        weight = weight + jnp.where(source_group[0] == g, group_weight[g], 0.0)
    scale = weight * (0.25 / math.sqrt(n_src * 2 * count))

    for f in range(count):
        index = frequency_index[h * count + f].astype(f32)
        value = math.log(2.0 * math.pi) + math.log(10.0) * (-1.0 + (4.0 / (2 * count - 1)) * index)
        log_omega[f] = jnp.full((size, LANES), value, f32)

    def chain_rule(g, r):
        sigma, chg, tau, expo = (
            params[pl.ds(8 * size * g + 2 * p + r, size, stride=8), :] for p in range(4)
        )
        sigma = jnp.exp(sigma) * scale
        angle = expo * (0.5 * math.pi)
        cosine, sine = jnp.cos(angle), jnp.sin(angle)
        rest = 1.0 - chg
        q_scale = sigma * chg
        log_product = log_omega[...] + tau
        amplitude = jnp.exp(expo * log_product)
        z_r, z_i = amplitude * cosine, amplitude * sine
        d_r, d_i = 1.0 + rest * z_r, rest * z_i
        inverse = 1.0 / (d_r * d_r + d_i * d_i)
        r_r, r_i = d_r * inverse, -d_i * inverse
        s_r, s_i = (1.0 + z_r) * r_r - z_i * r_i, (1.0 + z_r) * r_i + z_i * r_r
        t_r, t_i = z_r * r_r - z_i * r_i, z_r * r_i + z_i * r_r
        s_r, s_i = sigma * s_r, sigma * s_i
        q_r, q_i = q_scale * (t_r * r_r - t_i * r_i), q_scale * (t_r * r_i + t_i * r_r)
        parts = (
            (s_r, s_i),
            (s_r * t_r - s_i * t_i, s_r * t_i + s_i * t_r),
            (expo * q_r, expo * q_i),
            (
                q_r * log_product - (0.5 * math.pi) * q_i,
                (0.5 * math.pi) * q_r + q_i * log_product,
            ),
        )
        return parts

    def with_x(g, r):
        ahead = rows.at[1] if r == 0 else from_next
        behind = from_prev if r == 0 else rows.at[0]
        f_r, f_i, a_r, a_i = (
            ahead[:, i, part(g), :] - behind[:, i, part(g), :] for i in range(4)
        )
        c_r = f_r * a_r - f_i * a_i + yz_corr[r, 0, :, part(g), :]
        c_i = f_r * a_i + f_i * a_r + yz_corr[r, 1, :, part(g), :]
        return c_r, c_i

    for g in range(groups):
        inside_group = s // places == g
        def wait_params(g=g, inside_group=inside_group):
            if places > 1:
                where_there(inside_group, lambda g=g: gathered(g, places - 1).wait_recv())
            where_there(jnp.logical_not(inside_group), lambda g=g: gathered(g, places).wait_recv())

        def wait_rows(g=g):
            where_there(has_prev, lambda g=g: up(g).wait_recv())
            where_there(has_next, lambda g=g: down(g).wait_recv())

        if g == 0:
            wait_rows()
            for r in range(2):
                c_r, c_i = with_x(g, r)
                yz_corr[r, 0, :, part(g), :], yz_corr[r, 1, :, part(g), :] = c_r, c_i
        wait_params()
        for r in range(2):
            parts = chain_rule(g, r)
            if g == 0:
                c_r, c_i = yz_corr[r, 0, :, part(g), :], yz_corr[r, 1, :, part(g), :]
                for p, (part_r, part_i) in enumerate(parts):
                    gradient = jnp.sum(part_r * c_r - part_i * c_i, axis=0)
                    partial[pl.ds(8 * size * g + 2 * p + r, size, stride=8), :] = gradient
            else:
                for p, (part_r, part_i) in enumerate(parts):
                    derivs[r, 2 * p] = part_r
                    derivs[r, 2 * p + 1] = part_i
        if g > 0:
            wait_rows()
            for r in range(2):
                c_r, c_i = with_x(g, r)
                for p in range(4):
                    gradient = jnp.sum(derivs[r, 2 * p] * c_r - derivs[r, 2 * p + 1] * c_i, axis=0)
                    partial[pl.ds(8 * size * g + 2 * p + r, size, stride=8), :] = gradient

        for i in range(places):
            to = places * g + lax.rem(s + i, places)

            @pl.when(s != to)
            def _():
                pltpu.make_async_remote_copy(
                    src_ref=partial.at[pl.ds(pl.multiple_of(16 * to, 16), 16)],
                    dst_ref=arrived.at[pair],
                    send_sem=scatter_sem.at[0],
                    recv_sem=scatter_sem.at[1],
                    device_id=(to, h, b),
                    device_id_type=MESH,
                ).start()

    to_partner(1).wait_recv()
    mask = masks[...]
    scattered = pltpu.make_async_remote_copy(
        src_ref=partial.at[others],
        dst_ref=arrived.at[others],
        send_sem=scatter_sem.at[0],
        recv_sem=scatter_sem.at[1],
        device_id=(along(1), h, b),
        device_id_type=MESH,
    )
    scattered.wait_recv()
    arrived[pair, :] = partial[pair, :]
    tiles = [arrived[pl.ds(16 * i, 16), :] for i in range(n_src)]
    while len(tiles) > 1:
        tiles = [
            tiles[i] + tiles[i + 1] if i + 1 < len(tiles) else tiles[i]
            for i in range(0, len(tiles), 2)
        ]
    window[in_window(1, h, 8 - 8 * h, 16), :] = tiles[0] * mask

    def to_near(entry):
        there, part, device, (start, length), slot, kind = sends[entry]
        return pltpu.make_async_remote_copy(
            src_ref=window.at[in_window(1, h, 8 - 8 * h + part, length)],
            dst_ref=window.at[in_window(slot, h, start, length)],
            send_sem=near_send.at[entry],
            recv_sem=near_recv.at[4 * slot + 2 * h + kind],
            device_id=device,
            device_id_type=MESH,
        )

    def from_near(entry):
        there, device, (start, length), slot, other, kind = receives[entry]
        part = window.at[in_window(slot, other, start, length)]
        return pltpu.make_async_remote_copy(
            src_ref=part,
            dst_ref=part,
            send_sem=near_send.at[0],
            recv_sem=near_recv.at[4 * slot + 2 * other + kind],
            device_id=device,
            device_id_type=MESH,
        )

    for entry in range(len(sends)):
        where_there(sends[entry][0], lambda entry=entry: to_near(entry).start())

    tile_lane = lax.broadcasted_iota(jnp.int32, (8, LANES), 1)
    tile_line = lax.broadcasted_iota(jnp.int32, (8, LANES), 0)
    tile_low = tile_lane < NY
    tile_y = jnp.bitwise_and(tile_lane, NY - 1)
    top, bottom = tile_y == NY - 1, tile_y == 0
    first_row = jnp.bitwise_and(tile_line, 1) == 0
    smooth = []
    for d in range(3):
        w = jnp.full((8, LANES), prior_weight[0, d], f32)
        for p in range(1, 4):
            w = jnp.where(tile_line >= 2 * p, prior_weight[p, d], w)
        smooth.append(w)

    def one_pass(mid, prev, after, lower, upper):
        x_sum = jnp.where(first_row, pltpu.roll(mid, 7, 0), pltpu.roll(after, 1, 0)) + jnp.where(
            first_row, pltpu.roll(prev, 7, 0), pltpu.roll(mid, 1, 0)
        )
        y_sum = jnp.where(top, 0.0, pltpu.roll(mid, LANES - 1, 1)) + jnp.where(
            bottom, 0.0, pltpu.roll(mid, 1, 1)
        )
        turned = pltpu.roll(mid, NY, 1)
        z_sum = jnp.where(tile_low, turned, pltpu.roll(upper, NY, 1)) + jnp.where(
            tile_low, pltpu.roll(lower, NY, 1), turned
        )
        twice = 2.0 * mid
        return (
            mid
            + smooth[0] * (x_sum - twice)
            + smooth[1] * (y_sum - twice)
            + smooth[2] * (z_sum - twice)
        )

    for g in range(groups):
        where_there(has_next, lambda g=g: up(g).wait_send())
        where_there(has_prev, lambda g=g: down(g).wait_send())
    to_partner(0).wait_send()
    to_partner(1).wait_send()
    gathered(0, n_src - 1).wait_send()
    scattered.wait_send()

    for entry in range(len(sends)):
        where_there(sends[entry][0], lambda entry=entry: to_near(entry).wait_send())

    for entry in range(len(receives)):
        where_there(receives[entry][0], lambda entry=entry: from_near(entry).wait_recv())

    def tile(db, dk):
        return sum(window[in_window(db + 1, other, 8 * (dk + 1), 8), :] for other in range(2))

    empty = jnp.zeros((8, LANES), f32)

    def inside(there, value):
        return jnp.where(there, value, 0.0)

    middle = tile(0, 0)
    mid = one_pass(middle, tile(-1, 0), tile(1, 0), tile(0, -1), tile(0, 1))
    prev = one_pass(tile(-1, 0), empty, middle, tile(-1, -1), tile(-1, 1))
    after = one_pass(tile(1, 0), middle, empty, tile(1, -1), tile(1, 1))
    lower = one_pass(tile(0, -1), tile(-1, -1), tile(1, -1), empty, middle)
    upper = one_pass(tile(0, 1), tile(-1, 1), tile(1, 1), middle, empty)
    out[...] = one_pass(
        mid,
        inside(has_prev, prev),
        inside(has_next, after),
        inside(k > 0, lower),
        inside(k < chunks - 1, upper),
    )


def solution(mesh):
    n_src, n_space = mesh.shape["src"], mesh.shape["space"]
    chunks = 2 * n_src

    def local(
        forward,
        adjoint,
        source_group,
        group_weight,
        frequency_index,
        log_sigma,
        charge,
        log_tau,
        exponent,
        active,
        prior_weight,
    ):
        count = forward.shape[1]
        size = min(8, chunks)
        groups = chunks // size

        def keep(x):
            return pltpu.with_memory_space_constraint(x, pltpu.HBM)

        def lines(field):
            split = field.reshape(count, 2, 2, chunks, LANES)
            return split.transpose(0, 1, 3, 2, 4).reshape(count, 4 * chunks, LANES)

        hbm = pl.BlockSpec(memory_space=pl.ANY)
        vmem = pl.BlockSpec(memory_space=pltpu.VMEM)
        smem = pl.BlockSpec(memory_space=pltpu.SMEM)
        f32 = jnp.float32
        result = pl.pallas_call(
            functools.partial(kernel, (n_src, n_space, count)),
            out_shape=jax.ShapeDtypeStruct((8, LANES), f32),
            in_specs=[hbm] * 7 + [smem] + [hbm] * 3,
            out_specs=vmem,
            scratch_shapes=[
                pltpu.VMEM((4, 2, LANES), f32),
                pltpu.VMEM((2, LANES), jnp.int32),
                pltpu.SMEM(group_weight.shape, f32),
                pltpu.SMEM(frequency_index.shape, jnp.int32),
                pltpu.SMEM(prior_weight.shape, f32),
                pltpu.VMEM((2, count, 4 * chunks, LANES), f32),
                pltpu.VMEM((2, count, 4, chunks, LANES), f32),
                pltpu.VMEM((count, 4, chunks, LANES), f32),
                pltpu.VMEM((count, 4, chunks, LANES), f32),
                pltpu.VMEM((8 * chunks, LANES), f32),
                pltpu.VMEM((16, LANES), f32),
                pltpu.VMEM((8 * chunks, LANES), f32),
                pltpu.VMEM((8 * chunks, LANES), f32),
                pltpu.VMEM((6 * 24, LANES), f32),
                pltpu.VMEM((2, 8, count, size, LANES), f32),
                pltpu.VMEM((2, 2, count, chunks, LANES), f32),
                pltpu.VMEM((count, size, LANES), f32),
                pltpu.SemaphoreType.DMA((2,)),
                pltpu.SemaphoreType.DMA((8,)),
                pltpu.SemaphoreType.DMA((2, groups)),
                pltpu.SemaphoreType.DMA((2, groups)),
                pltpu.SemaphoreType.DMA((2,)),
                pltpu.SemaphoreType.DMA((2,)),
                pltpu.SemaphoreType.DMA((1 + groups,)),
                pltpu.SemaphoreType.DMA((2,)),
                pltpu.SemaphoreType.DMA((11,)),
                pltpu.SemaphoreType.DMA((12,)),
                pltpu.SemaphoreType.REGULAR,
                pltpu.SemaphoreType.REGULAR,
            ],
            compiler_params=pltpu.CompilerParams(
                collective_id=0, has_side_effects=True, vmem_limit_bytes=32 * 1024 * 1024
            ),
        )(
            *map(keep, (lines(forward), lines(adjoint), log_sigma, charge, log_tau, exponent, active)),
            source_group,
            *map(keep, (group_weight, frequency_index, prior_weight)),
        )
        return result.reshape(4, 2, LANES)

    placed = (
        P("src", "freq", None, "space", None),
        P("src", "freq", None, "space", None),
        P("src"),
        P(),
        P(),
        P("space", ("src", "freq")),
        P("space", ("src", "freq")),
        P("space", ("src", "freq")),
        P("space", ("src", "freq")),
        P("space", ("src", "freq")),
        P(),
    )
    return jax.shard_map(
        local,
        mesh=mesh,
        in_specs=placed,
        out_specs=P(None, "space", ("src", "freq")),
        check_vma=False,
    )
```

```python
import functools
import math

import jax
import jax.numpy as jnp
from jax import lax
from jax.experimental import pallas as pl
from jax.experimental.pallas import tpu as pltpu
from jax.sharding import PartitionSpec as P

MESH = pl.DeviceIdType.MESH
GROUPS = 3
NY = 64
LANES = 128


def kernel(
    sizes,
    forward,
    adjoint,
    log_sigma,
    charge,
    log_tau,
    exponent,
    active_in,
    source_group,
    group_weight_in,
    frequency_index_in,
    prior_weight_in,
    out,
    cell_params,
    active,
    group_weight,
    frequency_index,
    prior_weight,
    own,
    rows,
    from_prev,
    from_next,
    params,
    masks,
    partial,
    arrived,
    window,
    derivs,
    yz_corr,
    log_omega,
    load_sem,
    small_sem,
    halo_send,
    halo_recv,
    pair_send,
    pair_recv,
    gather_sem,
    scatter_sem,
    near_send,
    near_recv,
    first_sem,
    second_sem,
):
    n_src, n_space, count = sizes
    chunks = 2 * n_src
    half = 2 * chunks
    size = min(8, chunks)
    groups = chunks // size
    places = size // 2
    s, h, b = lax.axis_index("src"), lax.axis_index("freq"), lax.axis_index("space")
    k = 2 * s + h
    f32 = jnp.float32
    steps = sorted(range(1, n_src), key=lambda step: -min(step, n_src - step))

    def along(step):
        return lax.rem(s + step, n_src)

    loads = [
        pltpu.make_async_copy(field, own.at[i, :, pl.ds(0, 2 * half), :], load_sem.at[i])
        for i, field in enumerate((forward, adjoint))
    ]
    small = [
        pltpu.make_async_copy(source, target, small_sem.at[i])
        for i, (source, target) in enumerate(
            (
                (log_sigma, cell_params.at[0]),
                (charge, cell_params.at[1]),
                (log_tau, cell_params.at[2]),
                (exponent, cell_params.at[3]),
                (active_in, active),
                (group_weight_in, group_weight),
                (frequency_index_in, frequency_index),
                (prior_weight_in, prior_weight),
            )
        )
    ]
    has_prev, has_next = b > 0, b < n_space - 1
    beside = {-1: has_prev, 0: None, 1: has_next}

    def both(first, second):
        if first is None or second is None:
            return second if first is None else first
        return jnp.logical_and(first, second)

    def in_window(slot, share, start, length):
        return pl.ds(pl.multiple_of(48 * slot + 24 * share + start, 8), length)

    def where_there(there, act):
        if there is None:
            act()
        else:
            pl.when(there)(act)

    side, away = s - 1 + 2 * h, s + 1 - 2 * h
    has_side = jnp.logical_and(side >= 0, side < n_src)
    has_away = jnp.logical_and(away >= 0, away < n_src)
    sends = []
    for db in (-1, 1, 0):
        there = both(has_side, beside[db])
        sends.append((there, 8 * h, (side, 1 - h, b + db), (16 - 16 * h, 8), 1 - db, 1))
        sends.append((beside[db], 0, (s, 1 - h, b + db), (8 * h, 16), 1 - db, 0))
    for db in (-1, 1, 0):
        there = both(has_away, beside[db])
        sends.append((there, 8 - 8 * h, (away, h, b + db), (16 * h, 8), 1 - db, 1))
        if db != 0:
            sends.append((beside[db], 0, (s, h, b + db), (8 - 8 * h, 16), 1 - db, 0))
    receives = []
    for db in (-1, 1):
        receives.append((beside[db], (s, h, b + db), (8 - 8 * h, 16), 1 + db, h, 0))
    for other in (h, 1 - h):
        for db in (0, -1, 1):
            there = both(has_side, beside[db])
            receives.append((there, (side, other, b + db), (16 * h, 8), 1 + db, other, 1))
    for db in (-1, 1, 0):
        receives.append((beside[db], (s, 1 - h, b + db), (8 - 8 * h, 16), 1 + db, 1 - h, 0))

    odd = lax.rem(b, 2)
    first_core, second_core = b - odd, b - odd + 1
    next_chip = first_core - 2 + 4 * odd
    has_chip = jnp.logical_and(next_chip >= 0, next_chip < n_space)
    barrier = pltpu.get_barrier_semaphore()

    def greet(*device):
        pl.semaphore_signal(barrier, inc=1, device_id=device, device_id_type=MESH)

    for step in steps:
        greet(along(step), h, second_core)
    where_there(odd == 1, functools.partial(greet, s, h, first_core))
    where_there(has_chip, functools.partial(greet, s, h, next_chip))
    greet(s, 1 - h, first_core)
    for load in loads + small:
        load.start()
    where_there(both(has_side, has_chip), functools.partial(greet, side, 1 - h, next_chip + 1))
    where_there(has_side, functools.partial(greet, side, 1 - h, second_core))
    where_there(has_chip, functools.partial(greet, s, 1 - h, next_chip + 1))
    where_there(both(has_side, has_chip), functools.partial(greet, side, h, next_chip + 1))

    chips = (first_core > 0).astype(jnp.int32) + (second_core < n_space - 1).astype(jnp.int32)
    to_side, to_away = has_side.astype(jnp.int32), has_away.astype(jnp.int32)
    first_count = 3 + chips
    second_count = 2 * (n_src - 1) + chips * (1 + to_side + to_away) + 2 * to_side

    mine = pl.ds(pl.multiple_of(8 * k, 8), 8)
    my_half = pl.ds(pl.multiple_of(8 * h, 8), 8)
    for load in small:
        load.wait()
    params[mine, :] = jnp.concatenate([cell_params[p] for p in range(4)], axis=0)
    masks[my_half, :] = jnp.concatenate([active[...].astype(f32)] * 4, axis=0)

    for load in loads:
        load.wait()

    def split_rows(f, carry):
        for i in range(2):
            for r in range(2):
                for c in range(2):
                    first = half * c + r
                    rows[r, f, 2 * i + c] = own[i, f, pl.ds(first, chunks, stride=2), :]
        return carry

    lax.fori_loop(0, count, split_rows, 0)

    @pl.when(jnp.logical_not(has_prev))
    def _():
        from_prev[...] = jnp.zeros_like(from_prev)
        window[pl.ds(0, 48), :] = jnp.zeros((48, LANES), f32)

    @pl.when(jnp.logical_not(has_next))
    def _():
        from_next[...] = jnp.zeros_like(from_next)
        window[pl.ds(96, 48), :] = jnp.zeros((48, LANES), f32)

    @pl.when(jnp.logical_not(has_side))
    def _():
        for db in range(3):
            for other in range(2):
                window[in_window(db, other, 16 * h, 8), :] = jnp.zeros((8, LANES), f32)

    @pl.when(odd == 0)
    def _():
        pl.semaphore_wait(barrier, first_count)
        pl.semaphore_signal(first_sem, inc=1, device_id=(s, h, second_core), device_id_type=MESH)

    @pl.when(odd == 1)
    def _():
        pl.semaphore_wait(first_sem, 1)

    def to_partner(i):
        ref, part = ((params, mine), (masks, my_half))[i]
        return pltpu.make_async_remote_copy(
            src_ref=ref.at[part],
            dst_ref=ref.at[part],
            send_sem=pair_send.at[i],
            recv_sem=pair_recv.at[i],
            device_id=(s, 1 - h, b),
            device_id_type=MESH,
        )

    to_partner(0).start()

    def part(g):
        return pl.ds(size * g, size)

    def up(g):
        return pltpu.make_async_remote_copy(
            src_ref=rows.at[1, :, :, part(g), :],
            dst_ref=from_prev.at[:, :, part(g), :],
            send_sem=halo_send.at[0, g],
            recv_sem=halo_recv.at[0, g],
            device_id=(s, h, b + 1),
            device_id_type=MESH,
        )

    def down(g):
        return pltpu.make_async_remote_copy(
            src_ref=rows.at[0, :, :, part(g), :],
            dst_ref=from_next.at[:, :, part(g), :],
            send_sem=halo_send.at[1, g],
            recv_sem=halo_recv.at[1, g],
            device_id=(s, h, b - 1),
            device_id_type=MESH,
        )

    for g in range(groups):
        where_there(has_next, lambda g=g: up(g).start())
        where_there(has_prev, lambda g=g: down(g).start())
    to_partner(1).start()

    lane = lax.broadcasted_iota(jnp.int32, (chunks, LANES), 1)
    line = lax.broadcasted_iota(jnp.int32, (chunks, LANES), 0)
    low = lane < NY
    y_pos = jnp.bitwise_and(lane, NY - 1)
    y_last, y_first = y_pos == NY - 1, y_pos == 0
    z_last, z_first = line == chunks - 1, line == 0

    def differences(u):
        grad_y = jnp.where(y_last, 0.0, pltpu.roll(u, LANES - 1, 1)) - jnp.where(
            y_first, 0.0, pltpu.roll(u, 1, 1)
        )
        turned = pltpu.roll(u, NY, 1)
        above = jnp.where(z_last, 0.0, pltpu.roll(turned, chunks - 1, 0))
        below = jnp.where(z_first, 0.0, pltpu.roll(turned, 1, 0))
        return grad_y, jnp.where(low, turned - below, above - turned)

    def correlate_yz(f, carry):
        for r in range(2):
            grads = [
                differences(rows[r, f, i]) for i in range(4)
            ]
            (fr_y, fr_z), (fi_y, fi_z), (ar_y, ar_z), (ai_y, ai_z) = grads
            yz_corr[r, 0, f] = fr_y * ar_y - fi_y * ai_y + (fr_z * ar_z - fi_z * ai_z)
            yz_corr[r, 1, f] = fr_y * ai_y + fi_y * ar_y + (fr_z * ai_z + fi_z * ar_z)
        return carry

    lax.fori_loop(0, count, correlate_yz, 0)

    @pl.when(odd == 1)
    def _():
        pl.semaphore_wait(barrier, second_count)
        pl.semaphore_signal(second_sem, inc=1, device_id=(s, h, first_core), device_id_type=MESH)

    @pl.when(odd == 0)
    def _():
        pl.semaphore_wait(second_sem, 1)

    to_partner(0).wait_recv()
    pair = pl.ds(pl.multiple_of(16 * s, 16), 16)
    for step in steps:
        pltpu.make_async_remote_copy(
            src_ref=params.at[pair],
            dst_ref=params.at[pair],
            send_sem=gather_sem.at[0],
            recv_sem=gather_sem.at[1 + s // places],
            device_id=(along(step), h, b),
            device_id_type=MESH,
        ).start()
    others = pl.ds(0, 16 * (n_src - 1))

    def gathered(g, count_of):
        there = pl.ds(0, 16 * count_of)
        return pltpu.make_async_remote_copy(
            src_ref=partial.at[there],
            dst_ref=params.at[there],
            send_sem=gather_sem.at[0],
            recv_sem=gather_sem.at[1 + g],
            device_id=(along(1), h, b),
            device_id_type=MESH,
        )

    weight = jnp.float32(0.0)
    for g in range(GROUPS):
        weight = weight + jnp.where(source_group[0] == g, group_weight[g], 0.0)
    scale = weight * (0.25 / math.sqrt(n_src * 2 * count))

    for f in range(count):
        index = frequency_index[h * count + f].astype(f32)
        value = math.log(2.0 * math.pi) + math.log(10.0) * (-1.0 + (4.0 / (2 * count - 1)) * index)
        log_omega[f] = jnp.full((size, LANES), value, f32)

    def chain_rule(g, r):
        sigma, chg, tau, expo = (
            params[pl.ds(8 * size * g + 2 * p + r, size, stride=8), :] for p in range(4)
        )
        sigma = jnp.exp(sigma) * scale
        angle = expo * (0.5 * math.pi)
        cosine, sine = jnp.cos(angle), jnp.sin(angle)
        rest = 1.0 - chg
        q_scale = sigma * chg
        log_product = log_omega[...] + tau
        amplitude = jnp.exp(expo * log_product)
        z_r, z_i = amplitude * cosine, amplitude * sine
        d_r, d_i = 1.0 + rest * z_r, rest * z_i
        inverse = 1.0 / (d_r * d_r + d_i * d_i)
        r_r, r_i = d_r * inverse, -d_i * inverse
        s_r, s_i = (1.0 + z_r) * r_r - z_i * r_i, (1.0 + z_r) * r_i + z_i * r_r
        t_r, t_i = z_r * r_r - z_i * r_i, z_r * r_i + z_i * r_r
        s_r, s_i = sigma * s_r, sigma * s_i
        q_r, q_i = q_scale * (t_r * r_r - t_i * r_i), q_scale * (t_r * r_i + t_i * r_r)
        parts = (
            (s_r, s_i),
            (s_r * t_r - s_i * t_i, s_r * t_i + s_i * t_r),
            (expo * q_r, expo * q_i),
            (
                q_r * log_product - (0.5 * math.pi) * q_i,
                (0.5 * math.pi) * q_r + q_i * log_product,
            ),
        )
        return parts

    def with_x(g, r):
        ahead = rows.at[1] if r == 0 else from_next
        behind = from_prev if r == 0 else rows.at[0]
        f_r, f_i, a_r, a_i = (
            ahead[:, i, part(g), :] - behind[:, i, part(g), :] for i in range(4)
        )
        c_r = f_r * a_r - f_i * a_i + yz_corr[r, 0, :, part(g), :]
        c_i = f_r * a_i + f_i * a_r + yz_corr[r, 1, :, part(g), :]
        return c_r, c_i

    for g in range(groups):
        inside_group = s // places == g
        def wait_params(g=g, inside_group=inside_group):
            if places > 1:
                where_there(inside_group, lambda g=g: gathered(g, places - 1).wait_recv())
            where_there(jnp.logical_not(inside_group), lambda g=g: gathered(g, places).wait_recv())

        def wait_rows(g=g):
            where_there(has_prev, lambda g=g: up(g).wait_recv())
            where_there(has_next, lambda g=g: down(g).wait_recv())

        if g == 0:
            wait_rows()
            for r in range(2):
                c_r, c_i = with_x(g, r)
                yz_corr[r, 0, :, part(g), :], yz_corr[r, 1, :, part(g), :] = c_r, c_i
        wait_params()
        for r in range(2):
            parts = chain_rule(g, r)
            if g == 0:
                c_r, c_i = yz_corr[r, 0, :, part(g), :], yz_corr[r, 1, :, part(g), :]
                for p, (part_r, part_i) in enumerate(parts):
                    gradient = jnp.sum(part_r * c_r - part_i * c_i, axis=0)
                    partial[pl.ds(8 * size * g + 2 * p + r, size, stride=8), :] = gradient
            else:
                for p, (part_r, part_i) in enumerate(parts):
                    derivs[r, 2 * p] = part_r
                    derivs[r, 2 * p + 1] = part_i
        if g > 0:
            wait_rows()
            for r in range(2):
                c_r, c_i = with_x(g, r)
                for p in range(4):
                    gradient = jnp.sum(derivs[r, 2 * p] * c_r - derivs[r, 2 * p + 1] * c_i, axis=0)
                    partial[pl.ds(8 * size * g + 2 * p + r, size, stride=8), :] = gradient

        for i in range(places):
            to = places * g + lax.rem(s + i, places)

            @pl.when(s != to)
            def _():
                pltpu.make_async_remote_copy(
                    src_ref=partial.at[pl.ds(pl.multiple_of(16 * to, 16), 16)],
                    dst_ref=arrived.at[pair],
                    send_sem=scatter_sem.at[0],
                    recv_sem=scatter_sem.at[1],
                    device_id=(to, h, b),
                    device_id_type=MESH,
                ).start()

    to_partner(1).wait_recv()
    mask = masks[...]
    scattered = pltpu.make_async_remote_copy(
        src_ref=partial.at[others],
        dst_ref=arrived.at[others],
        send_sem=scatter_sem.at[0],
        recv_sem=scatter_sem.at[1],
        device_id=(along(1), h, b),
        device_id_type=MESH,
    )
    scattered.wait_recv()
    arrived[pair, :] = partial[pair, :]
    tiles = [arrived[pl.ds(16 * i, 16), :] for i in range(n_src)]
    while len(tiles) > 1:
        tiles = [
            tiles[i] + tiles[i + 1] if i + 1 < len(tiles) else tiles[i]
            for i in range(0, len(tiles), 2)
        ]
    window[in_window(1, h, 8 - 8 * h, 16), :] = tiles[0] * mask

    def to_near(entry):
        there, part, device, (start, length), slot, kind = sends[entry]
        return pltpu.make_async_remote_copy(
            src_ref=window.at[in_window(1, h, 8 - 8 * h + part, length)],
            dst_ref=window.at[in_window(slot, h, start, length)],
            send_sem=near_send.at[entry],
            recv_sem=near_recv.at[4 * slot + 2 * h + kind],
            device_id=device,
            device_id_type=MESH,
        )

    def from_near(entry):
        there, device, (start, length), slot, other, kind = receives[entry]
        part = window.at[in_window(slot, other, start, length)]
        return pltpu.make_async_remote_copy(
            src_ref=part,
            dst_ref=part,
            send_sem=near_send.at[0],
            recv_sem=near_recv.at[4 * slot + 2 * other + kind],
            device_id=device,
            device_id_type=MESH,
        )

    for entry in range(len(sends)):
        where_there(sends[entry][0], lambda entry=entry: to_near(entry).start())

    tile_lane = lax.broadcasted_iota(jnp.int32, (8, LANES), 1)
    tile_line = lax.broadcasted_iota(jnp.int32, (8, LANES), 0)
    tile_low = tile_lane < NY
    tile_y = jnp.bitwise_and(tile_lane, NY - 1)
    top, bottom = tile_y == NY - 1, tile_y == 0
    first_row = jnp.bitwise_and(tile_line, 1) == 0
    smooth = []
    for d in range(3):
        w = jnp.full((8, LANES), prior_weight[0, d], f32)
        for p in range(1, 4):
            w = jnp.where(tile_line >= 2 * p, prior_weight[p, d], w)
        smooth.append(w)

    def one_pass(mid, prev, after, lower, upper):
        x_sum = jnp.where(first_row, pltpu.roll(mid, 7, 0), pltpu.roll(after, 1, 0)) + jnp.where(
            first_row, pltpu.roll(prev, 7, 0), pltpu.roll(mid, 1, 0)
        )
        y_sum = jnp.where(top, 0.0, pltpu.roll(mid, LANES - 1, 1)) + jnp.where(
            bottom, 0.0, pltpu.roll(mid, 1, 1)
        )
        turned = pltpu.roll(mid, NY, 1)
        z_sum = jnp.where(tile_low, turned, pltpu.roll(upper, NY, 1)) + jnp.where(
            tile_low, pltpu.roll(lower, NY, 1), turned
        )
        twice = 2.0 * mid
        return (
            mid
            + smooth[0] * (x_sum - twice)
            + smooth[1] * (y_sum - twice)
            + smooth[2] * (z_sum - twice)
        )

    for g in range(groups):
        where_there(has_next, lambda g=g: up(g).wait_send())
        where_there(has_prev, lambda g=g: down(g).wait_send())
    to_partner(0).wait_send()
    to_partner(1).wait_send()
    gathered(0, n_src - 1).wait_send()
    scattered.wait_send()

    for entry in range(len(sends)):
        where_there(sends[entry][0], lambda entry=entry: to_near(entry).wait_send())

    for entry in range(len(receives)):
        where_there(receives[entry][0], lambda entry=entry: from_near(entry).wait_recv())

    def tile(db, dk):
        return sum(window[in_window(db + 1, other, 8 * (dk + 1), 8), :] for other in range(2))

    empty = jnp.zeros((8, LANES), f32)

    def inside(there, value):
        return jnp.where(there, value, 0.0)

    middle = tile(0, 0)
    mid = one_pass(middle, tile(-1, 0), tile(1, 0), tile(0, -1), tile(0, 1))
    prev = one_pass(tile(-1, 0), empty, middle, tile(-1, -1), tile(-1, 1))
    after = one_pass(tile(1, 0), middle, empty, tile(1, -1), tile(1, 1))
    lower = one_pass(tile(0, -1), tile(-1, -1), tile(1, -1), empty, middle)
    upper = one_pass(tile(0, 1), tile(-1, 1), tile(1, 1), middle, empty)
    out[...] = one_pass(
        mid,
        inside(has_prev, prev),
        inside(has_next, after),
        inside(k > 0, lower),
        inside(k < chunks - 1, upper),
    )


def solution(mesh):
    n_src, n_space = mesh.shape["src"], mesh.shape["space"]
    chunks = 2 * n_src

    def local(
        forward,
        adjoint,
        source_group,
        group_weight,
        frequency_index,
        log_sigma,
        charge,
        log_tau,
        exponent,
        active,
        prior_weight,
    ):
        count = forward.shape[1]
        size = min(8, chunks)
        groups = chunks // size

        def keep(x):
            return pltpu.with_memory_space_constraint(x, pltpu.HBM)

        def lines(field):
            split = field.reshape(count, 2, 2, chunks, LANES)
            return split.transpose(0, 1, 3, 2, 4).reshape(count, 4 * chunks, LANES)

        hbm = pl.BlockSpec(memory_space=pl.ANY)
        vmem = pl.BlockSpec(memory_space=pltpu.VMEM)
        smem = pl.BlockSpec(memory_space=pltpu.SMEM)
        f32 = jnp.float32
        result = pl.pallas_call(
            functools.partial(kernel, (n_src, n_space, count)),
            out_shape=jax.ShapeDtypeStruct((8, LANES), f32),
            in_specs=[hbm] * 7 + [smem] + [hbm] * 3,
            out_specs=vmem,
            scratch_shapes=[
                pltpu.VMEM((4, 2, LANES), f32),
                pltpu.VMEM((2, LANES), jnp.int32),
                pltpu.SMEM(group_weight.shape, f32),
                pltpu.SMEM(frequency_index.shape, jnp.int32),
                pltpu.SMEM(prior_weight.shape, f32),
                pltpu.VMEM((2, count, 4 * chunks + 8, LANES), f32),
                pltpu.VMEM((2, count, 4, chunks, LANES), f32),
                pltpu.VMEM((count, 4, chunks, LANES), f32),
                pltpu.VMEM((count, 4, chunks, LANES), f32),
                pltpu.VMEM((8 * chunks + 8, LANES), f32),
                pltpu.VMEM((16, LANES), f32),
                pltpu.VMEM((8 * chunks + 8, LANES), f32),
                pltpu.VMEM((8 * chunks, LANES), f32),
                pltpu.VMEM((6 * 24, LANES), f32),
                pltpu.VMEM((2, 8, count, size, LANES), f32),
                pltpu.VMEM((2, 2, count, chunks, LANES), f32),
                pltpu.VMEM((count, size, LANES), f32),
                pltpu.SemaphoreType.DMA((2,)),
                pltpu.SemaphoreType.DMA((8,)),
                pltpu.SemaphoreType.DMA((2, groups)),
                pltpu.SemaphoreType.DMA((2, groups)),
                pltpu.SemaphoreType.DMA((2,)),
                pltpu.SemaphoreType.DMA((2,)),
                pltpu.SemaphoreType.DMA((1 + groups,)),
                pltpu.SemaphoreType.DMA((2,)),
                pltpu.SemaphoreType.DMA((11,)),
                pltpu.SemaphoreType.DMA((12,)),
                pltpu.SemaphoreType.REGULAR,
                pltpu.SemaphoreType.REGULAR,
            ],
            compiler_params=pltpu.CompilerParams(
                collective_id=0, has_side_effects=True, vmem_limit_bytes=32 * 1024 * 1024
            ),
        )(
            *map(keep, (lines(forward), lines(adjoint), log_sigma, charge, log_tau, exponent, active)),
            source_group,
            *map(keep, (group_weight, frequency_index, prior_weight)),
        )
        return result.reshape(4, 2, LANES)

    placed = (
        P("src", "freq", None, "space", None),
        P("src", "freq", None, "space", None),
        P("src"),
        P(),
        P(),
        P("space", ("src", "freq")),
        P("space", ("src", "freq")),
        P("space", ("src", "freq")),
        P("space", ("src", "freq")),
        P("space", ("src", "freq")),
        P(),
    )
    return jax.shard_map(
        local,
        mesh=mesh,
        in_specs=placed,
        out_specs=P(None, "space", ("src", "freq")),
        check_vma=False,
    )
```

```python
import functools
import math

import jax
import jax.numpy as jnp
from jax import lax
from jax.experimental import pallas as pl
from jax.experimental.pallas import tpu as pltpu
from jax.sharding import PartitionSpec as P

MESH = pl.DeviceIdType.MESH
GROUPS = 3
NY = 64
LANES = 128


def kernel(
    sizes,
    forward,
    adjoint,
    log_sigma,
    charge,
    log_tau,
    exponent,
    active_in,
    source_group,
    group_weight_in,
    frequency_index_in,
    prior_weight_in,
    out,
    cell_params,
    active,
    group_weight,
    frequency_index,
    prior_weight,
    own,
    rows,
    from_prev,
    from_next,
    params,
    masks,
    partial,
    arrived,
    window,
    derivs,
    yz_corr,
    log_omega,
    load_sem,
    small_sem,
    halo_send,
    halo_recv,
    pair_send,
    pair_recv,
    gather_sem,
    scatter_sem,
    near_send,
    near_recv,
    first_sem,
    second_sem,
):
    n_src, n_space, count = sizes
    chunks = 2 * n_src
    half = 2 * chunks
    size = min(8, chunks)
    groups = chunks // size
    places = size // 2
    s, h, b = lax.axis_index("src"), lax.axis_index("freq"), lax.axis_index("space")
    k = 2 * s + h
    f32 = jnp.float32
    steps = sorted(range(1, n_src), key=lambda step: -min(step, n_src - step))

    def along(step):
        return lax.rem(s + step, n_src)

    loads = [
        pltpu.make_async_copy(field, own.at[i, :, pl.ds(0, 2 * half), :], load_sem.at[i])
        for i, field in enumerate((forward, adjoint))
    ]
    small = [
        pltpu.make_async_copy(source, target, small_sem.at[i])
        for i, (source, target) in enumerate(
            (
                (log_sigma, cell_params.at[0]),
                (charge, cell_params.at[1]),
                (log_tau, cell_params.at[2]),
                (exponent, cell_params.at[3]),
                (active_in, active),
                (group_weight_in, group_weight),
                (frequency_index_in, frequency_index),
                (prior_weight_in, prior_weight),
            )
        )
    ]
    has_prev, has_next = b > 0, b < n_space - 1
    beside = {-1: has_prev, 0: None, 1: has_next}

    def both(first, second):
        if first is None or second is None:
            return second if first is None else first
        return jnp.logical_and(first, second)

    def in_window(slot, share, start, length):
        return pl.ds(pl.multiple_of(48 * slot + 24 * share + start, 8), length)

    def where_there(there, act):
        if there is None:
            act()
        else:
            pl.when(there)(act)

    side, away = s - 1 + 2 * h, s + 1 - 2 * h
    has_side = jnp.logical_and(side >= 0, side < n_src)
    has_away = jnp.logical_and(away >= 0, away < n_src)
    sends = []
    for db in (-1, 1, 0):
        there = both(has_side, beside[db])
        sends.append((there, 8 * h, (side, 1 - h, b + db), (16 - 16 * h, 8), 1 - db, 1))
        sends.append((beside[db], 0, (s, 1 - h, b + db), (8 * h, 16), 1 - db, 0))
    for db in (-1, 1, 0):
        there = both(has_away, beside[db])
        sends.append((there, 8 - 8 * h, (away, h, b + db), (16 * h, 8), 1 - db, 1))
        if db != 0:
            sends.append((beside[db], 0, (s, h, b + db), (8 - 8 * h, 16), 1 - db, 0))
    receives = []
    for db in (-1, 1):
        receives.append((beside[db], (s, h, b + db), (8 - 8 * h, 16), 1 + db, h, 0))
    for other in (h, 1 - h):
        for db in (0, -1, 1):
            there = both(has_side, beside[db])
            receives.append((there, (side, other, b + db), (16 * h, 8), 1 + db, other, 1))
    for db in (-1, 1, 0):
        receives.append((beside[db], (s, 1 - h, b + db), (8 - 8 * h, 16), 1 + db, 1 - h, 0))

    odd = lax.rem(b, 2)
    first_core, second_core = b - odd, b - odd + 1
    next_chip = first_core - 2 + 4 * odd
    has_chip = jnp.logical_and(next_chip >= 0, next_chip < n_space)
    barrier = pltpu.get_barrier_semaphore()

    def greet(*device):
        pl.semaphore_signal(barrier, inc=1, device_id=device, device_id_type=MESH)

    for step in steps:
        greet(along(step), h, second_core)
    where_there(odd == 1, functools.partial(greet, s, h, first_core))
    where_there(has_chip, functools.partial(greet, s, h, next_chip))
    greet(s, 1 - h, first_core)
    for load in loads + small:
        load.start()
    where_there(both(has_side, has_chip), functools.partial(greet, side, 1 - h, next_chip + 1))
    where_there(has_side, functools.partial(greet, side, 1 - h, second_core))
    where_there(has_chip, functools.partial(greet, s, 1 - h, next_chip + 1))
    where_there(both(has_side, has_chip), functools.partial(greet, side, h, next_chip + 1))

    chips = (first_core > 0).astype(jnp.int32) + (second_core < n_space - 1).astype(jnp.int32)
    to_side, to_away = has_side.astype(jnp.int32), has_away.astype(jnp.int32)
    first_count = 3 + chips
    second_count = 2 * (n_src - 1) + chips * (1 + to_side + to_away) + 2 * to_side

    mine = pl.ds(pl.multiple_of(8 * k, 8), 8)
    my_half = pl.ds(pl.multiple_of(8 * h, 8), 8)
    for load in small:
        load.wait()
    params[mine, :] = jnp.concatenate([cell_params[p] for p in range(4)], axis=0)
    masks[my_half, :] = jnp.concatenate([active[...].astype(f32)] * 4, axis=0)

    for load in loads:
        load.wait()

    def split_rows(f, carry):
        for i in range(2):
            for r in range(2):
                for c in range(2):
                    first = half * c + r
                    rows[r, f, 2 * i + c] = own[i, f, pl.ds(first, chunks, stride=2), :]
        return carry

    lax.fori_loop(0, count, split_rows, 0)

    @pl.when(jnp.logical_not(has_prev))
    def _():
        from_prev[...] = jnp.zeros_like(from_prev)
        window[pl.ds(0, 48), :] = jnp.zeros((48, LANES), f32)

    @pl.when(jnp.logical_not(has_next))
    def _():
        from_next[...] = jnp.zeros_like(from_next)
        window[pl.ds(96, 48), :] = jnp.zeros((48, LANES), f32)

    @pl.when(jnp.logical_not(has_side))
    def _():
        for db in range(3):
            for other in range(2):
                window[in_window(db, other, 16 * h, 8), :] = jnp.zeros((8, LANES), f32)

    @pl.when(odd == 0)
    def _():
        pl.semaphore_wait(barrier, first_count)
        pl.semaphore_signal(first_sem, inc=1, device_id=(s, h, second_core), device_id_type=MESH)

    @pl.when(odd == 1)
    def _():
        pl.semaphore_wait(first_sem, 1)

    def to_partner(i):
        ref, part = ((params, mine), (masks, my_half))[i]
        return pltpu.make_async_remote_copy(
            src_ref=ref.at[part],
            dst_ref=ref.at[part],
            send_sem=pair_send.at[i],
            recv_sem=pair_recv.at[i],
            device_id=(s, 1 - h, b),
            device_id_type=MESH,
        )

    to_partner(0).start()

    def part(g):
        return pl.ds(size * g, size)

    def up(g):
        return pltpu.make_async_remote_copy(
            src_ref=rows.at[1, :, :, part(g), :],
            dst_ref=from_prev.at[:, :, part(g), :],
            send_sem=halo_send.at[0, g],
            recv_sem=halo_recv.at[0, g],
            device_id=(s, h, b + 1),
            device_id_type=MESH,
        )

    def down(g):
        return pltpu.make_async_remote_copy(
            src_ref=rows.at[0, :, :, part(g), :],
            dst_ref=from_next.at[:, :, part(g), :],
            send_sem=halo_send.at[1, g],
            recv_sem=halo_recv.at[1, g],
            device_id=(s, h, b - 1),
            device_id_type=MESH,
        )

    for g in range(groups):
        where_there(has_next, lambda g=g: up(g).start())
        where_there(has_prev, lambda g=g: down(g).start())
    to_partner(1).start()

    lane = lax.broadcasted_iota(jnp.int32, (chunks, LANES), 1)
    line = lax.broadcasted_iota(jnp.int32, (chunks, LANES), 0)
    low = lane < NY
    y_pos = jnp.bitwise_and(lane, NY - 1)
    y_last, y_first = y_pos == NY - 1, y_pos == 0
    z_last, z_first = line == chunks - 1, line == 0

    def differences(u):
        grad_y = jnp.where(y_last, 0.0, pltpu.roll(u, LANES - 1, 1)) - jnp.where(
            y_first, 0.0, pltpu.roll(u, 1, 1)
        )
        turned = pltpu.roll(u, NY, 1)
        above = jnp.where(z_last, 0.0, pltpu.roll(turned, chunks - 1, 0))
        below = jnp.where(z_first, 0.0, pltpu.roll(turned, 1, 0))
        return grad_y, jnp.where(low, turned - below, above - turned)

    def correlate_yz(f, carry):
        for r in range(2):
            grads = [
                differences(rows[r, f, i]) for i in range(4)
            ]
            (fr_y, fr_z), (fi_y, fi_z), (ar_y, ar_z), (ai_y, ai_z) = grads
            yz_corr[r, 0, f] = fr_y * ar_y - fi_y * ai_y + (fr_z * ar_z - fi_z * ai_z)
            yz_corr[r, 1, f] = fr_y * ai_y + fi_y * ar_y + (fr_z * ai_z + fi_z * ar_z)
        return carry

    lax.fori_loop(0, count, correlate_yz, 0)

    weight = jnp.float32(0.0)
    for g in range(GROUPS):
        weight = weight + jnp.where(source_group[0] == g, group_weight[g], 0.0)
    scale = weight * (0.25 / math.sqrt(n_src * 2 * count))

    for f in range(count):
        index = frequency_index[h * count + f].astype(f32)
        value = math.log(2.0 * math.pi) + math.log(10.0) * (-1.0 + (4.0 / (2 * count - 1)) * index)
        log_omega[f] = jnp.full((size, LANES), value, f32)

    @pl.when(odd == 1)
    def _():
        pl.semaphore_wait(barrier, second_count)
        pl.semaphore_signal(second_sem, inc=1, device_id=(s, h, first_core), device_id_type=MESH)

    @pl.when(odd == 0)
    def _():
        pl.semaphore_wait(second_sem, 1)

    to_partner(0).wait_recv()
    pair = pl.ds(pl.multiple_of(16 * s, 16), 16)
    for step in steps:
        pltpu.make_async_remote_copy(
            src_ref=params.at[pair],
            dst_ref=params.at[pair],
            send_sem=gather_sem.at[0],
            recv_sem=gather_sem.at[1 + s // places],
            device_id=(along(step), h, b),
            device_id_type=MESH,
        ).start()
    others = pl.ds(0, 16 * (n_src - 1))

    def gathered(g, count_of):
        there = pl.ds(0, 16 * count_of)
        return pltpu.make_async_remote_copy(
            src_ref=partial.at[there],
            dst_ref=params.at[there],
            send_sem=gather_sem.at[0],
            recv_sem=gather_sem.at[1 + g],
            device_id=(along(1), h, b),
            device_id_type=MESH,
        )

    def chain_rule(g, r):
        sigma, chg, tau, expo = (
            params[pl.ds(8 * size * g + 2 * p + r, size, stride=8), :] for p in range(4)
        )
        sigma = jnp.exp(sigma) * scale
        angle = expo * (0.5 * math.pi)
        cosine, sine = jnp.cos(angle), jnp.sin(angle)
        rest = 1.0 - chg
        q_scale = sigma * chg
        log_product = log_omega[...] + tau
        amplitude = jnp.exp(expo * log_product)
        z_r, z_i = amplitude * cosine, amplitude * sine
        d_r, d_i = 1.0 + rest * z_r, rest * z_i
        inverse = 1.0 / (d_r * d_r + d_i * d_i)
        r_r, r_i = d_r * inverse, -d_i * inverse
        s_r, s_i = (1.0 + z_r) * r_r - z_i * r_i, (1.0 + z_r) * r_i + z_i * r_r
        t_r, t_i = z_r * r_r - z_i * r_i, z_r * r_i + z_i * r_r
        s_r, s_i = sigma * s_r, sigma * s_i
        q_r, q_i = q_scale * (t_r * r_r - t_i * r_i), q_scale * (t_r * r_i + t_i * r_r)
        parts = (
            (s_r, s_i),
            (s_r * t_r - s_i * t_i, s_r * t_i + s_i * t_r),
            (expo * q_r, expo * q_i),
            (
                q_r * log_product - (0.5 * math.pi) * q_i,
                (0.5 * math.pi) * q_r + q_i * log_product,
            ),
        )
        return parts

    def with_x(g, r):
        ahead = rows.at[1] if r == 0 else from_next
        behind = from_prev if r == 0 else rows.at[0]
        f_r, f_i, a_r, a_i = (
            ahead[:, i, part(g), :] - behind[:, i, part(g), :] for i in range(4)
        )
        c_r = f_r * a_r - f_i * a_i + yz_corr[r, 0, :, part(g), :]
        c_i = f_r * a_i + f_i * a_r + yz_corr[r, 1, :, part(g), :]
        return c_r, c_i

    for g in range(groups):
        inside_group = s // places == g
        def wait_params(g=g, inside_group=inside_group):
            if places > 1:
                where_there(inside_group, lambda g=g: gathered(g, places - 1).wait_recv())
            where_there(jnp.logical_not(inside_group), lambda g=g: gathered(g, places).wait_recv())

        def wait_rows(g=g):
            where_there(has_prev, lambda g=g: up(g).wait_recv())
            where_there(has_next, lambda g=g: down(g).wait_recv())

        if g == 0:
            wait_rows()
            for r in range(2):
                c_r, c_i = with_x(g, r)
                yz_corr[r, 0, :, part(g), :], yz_corr[r, 1, :, part(g), :] = c_r, c_i
        wait_params()
        for r in range(2):
            parts = chain_rule(g, r)
            if g == 0:
                c_r, c_i = yz_corr[r, 0, :, part(g), :], yz_corr[r, 1, :, part(g), :]
                for p, (part_r, part_i) in enumerate(parts):
                    gradient = jnp.sum(part_r * c_r - part_i * c_i, axis=0)
                    partial[pl.ds(8 * size * g + 2 * p + r, size, stride=8), :] = gradient
            else:
                for p, (part_r, part_i) in enumerate(parts):
                    derivs[r, 2 * p] = part_r
                    derivs[r, 2 * p + 1] = part_i
        if g > 0:
            wait_rows()
            for r in range(2):
                c_r, c_i = with_x(g, r)
                for p in range(4):
                    gradient = jnp.sum(derivs[r, 2 * p] * c_r - derivs[r, 2 * p + 1] * c_i, axis=0)
                    partial[pl.ds(8 * size * g + 2 * p + r, size, stride=8), :] = gradient

        for i in range(places):
            to = places * g + lax.rem(s + i, places)

            @pl.when(s != to)
            def _():
                pltpu.make_async_remote_copy(
                    src_ref=partial.at[pl.ds(pl.multiple_of(16 * to, 16), 16)],
                    dst_ref=arrived.at[pair],
                    send_sem=scatter_sem.at[0],
                    recv_sem=scatter_sem.at[1],
                    device_id=(to, h, b),
                    device_id_type=MESH,
                ).start()

    to_partner(1).wait_recv()
    mask = masks[...]
    scattered = pltpu.make_async_remote_copy(
        src_ref=partial.at[others],
        dst_ref=arrived.at[others],
        send_sem=scatter_sem.at[0],
        recv_sem=scatter_sem.at[1],
        device_id=(along(1), h, b),
        device_id_type=MESH,
    )
    scattered.wait_recv()
    arrived[pair, :] = partial[pair, :]
    tiles = [arrived[pl.ds(16 * i, 16), :] for i in range(n_src)]
    while len(tiles) > 1:
        tiles = [
            tiles[i] + tiles[i + 1] if i + 1 < len(tiles) else tiles[i]
            for i in range(0, len(tiles), 2)
        ]
    window[in_window(1, h, 8 - 8 * h, 16), :] = tiles[0] * mask

    def to_near(entry):
        there, part, device, (start, length), slot, kind = sends[entry]
        return pltpu.make_async_remote_copy(
            src_ref=window.at[in_window(1, h, 8 - 8 * h + part, length)],
            dst_ref=window.at[in_window(slot, h, start, length)],
            send_sem=near_send.at[entry],
            recv_sem=near_recv.at[4 * slot + 2 * h + kind],
            device_id=device,
            device_id_type=MESH,
        )

    def from_near(entry):
        there, device, (start, length), slot, other, kind = receives[entry]
        part = window.at[in_window(slot, other, start, length)]
        return pltpu.make_async_remote_copy(
            src_ref=part,
            dst_ref=part,
            send_sem=near_send.at[0],
            recv_sem=near_recv.at[4 * slot + 2 * other + kind],
            device_id=device,
            device_id_type=MESH,
        )

    for entry in range(len(sends)):
        where_there(sends[entry][0], lambda entry=entry: to_near(entry).start())

    tile_lane = lax.broadcasted_iota(jnp.int32, (8, LANES), 1)
    tile_line = lax.broadcasted_iota(jnp.int32, (8, LANES), 0)
    tile_low = tile_lane < NY
    tile_y = jnp.bitwise_and(tile_lane, NY - 1)
    top, bottom = tile_y == NY - 1, tile_y == 0
    first_row = jnp.bitwise_and(tile_line, 1) == 0
    smooth = []
    for d in range(3):
        w = jnp.full((8, LANES), prior_weight[0, d], f32)
        for p in range(1, 4):
            w = jnp.where(tile_line >= 2 * p, prior_weight[p, d], w)
        smooth.append(w)

    def one_pass(mid, prev, after, lower, upper):
        x_sum = jnp.where(first_row, pltpu.roll(mid, 7, 0), pltpu.roll(after, 1, 0)) + jnp.where(
            first_row, pltpu.roll(prev, 7, 0), pltpu.roll(mid, 1, 0)
        )
        y_sum = jnp.where(top, 0.0, pltpu.roll(mid, LANES - 1, 1)) + jnp.where(
            bottom, 0.0, pltpu.roll(mid, 1, 1)
        )
        turned = pltpu.roll(mid, NY, 1)
        z_sum = jnp.where(tile_low, turned, pltpu.roll(upper, NY, 1)) + jnp.where(
            tile_low, pltpu.roll(lower, NY, 1), turned
        )
        twice = 2.0 * mid
        return (
            mid
            + smooth[0] * (x_sum - twice)
            + smooth[1] * (y_sum - twice)
            + smooth[2] * (z_sum - twice)
        )

    for g in range(groups):
        where_there(has_next, lambda g=g: up(g).wait_send())
        where_there(has_prev, lambda g=g: down(g).wait_send())
    to_partner(0).wait_send()
    to_partner(1).wait_send()
    gathered(0, n_src - 1).wait_send()
    scattered.wait_send()

    for entry in range(len(sends)):
        where_there(sends[entry][0], lambda entry=entry: to_near(entry).wait_send())

    for entry in range(len(receives)):
        where_there(receives[entry][0], lambda entry=entry: from_near(entry).wait_recv())

    def tile(db, dk):
        return sum(window[in_window(db + 1, other, 8 * (dk + 1), 8), :] for other in range(2))

    empty = jnp.zeros((8, LANES), f32)

    def inside(there, value):
        return jnp.where(there, value, 0.0)

    middle = tile(0, 0)
    mid = one_pass(middle, tile(-1, 0), tile(1, 0), tile(0, -1), tile(0, 1))
    prev = one_pass(tile(-1, 0), empty, middle, tile(-1, -1), tile(-1, 1))
    after = one_pass(tile(1, 0), middle, empty, tile(1, -1), tile(1, 1))
    lower = one_pass(tile(0, -1), tile(-1, -1), tile(1, -1), empty, middle)
    upper = one_pass(tile(0, 1), tile(-1, 1), tile(1, 1), middle, empty)
    out[...] = one_pass(
        mid,
        inside(has_prev, prev),
        inside(has_next, after),
        inside(k > 0, lower),
        inside(k < chunks - 1, upper),
    )


def solution(mesh):
    n_src, n_space = mesh.shape["src"], mesh.shape["space"]
    chunks = 2 * n_src

    def local(
        forward,
        adjoint,
        source_group,
        group_weight,
        frequency_index,
        log_sigma,
        charge,
        log_tau,
        exponent,
        active,
        prior_weight,
    ):
        count = forward.shape[1]
        size = min(8, chunks)
        groups = chunks // size

        def keep(x):
            return pltpu.with_memory_space_constraint(x, pltpu.HBM)

        def lines(field):
            split = field.reshape(count, 2, 2, chunks, LANES)
            return split.transpose(0, 1, 3, 2, 4).reshape(count, 4 * chunks, LANES)

        hbm = pl.BlockSpec(memory_space=pl.ANY)
        vmem = pl.BlockSpec(memory_space=pltpu.VMEM)
        smem = pl.BlockSpec(memory_space=pltpu.SMEM)
        f32 = jnp.float32
        result = pl.pallas_call(
            functools.partial(kernel, (n_src, n_space, count)),
            out_shape=jax.ShapeDtypeStruct((8, LANES), f32),
            in_specs=[hbm] * 7 + [smem] + [hbm] * 3,
            out_specs=vmem,
            scratch_shapes=[
                pltpu.VMEM((4, 2, LANES), f32),
                pltpu.VMEM((2, LANES), jnp.int32),
                pltpu.SMEM(group_weight.shape, f32),
                pltpu.SMEM(frequency_index.shape, jnp.int32),
                pltpu.SMEM(prior_weight.shape, f32),
                pltpu.VMEM((2, count, 4 * chunks + 8, LANES), f32),
                pltpu.VMEM((2, count, 4, chunks, LANES), f32),
                pltpu.VMEM((count, 4, chunks, LANES), f32),
                pltpu.VMEM((count, 4, chunks, LANES), f32),
                pltpu.VMEM((8 * chunks + 8, LANES), f32),
                pltpu.VMEM((16, LANES), f32),
                pltpu.VMEM((8 * chunks + 8, LANES), f32),
                pltpu.VMEM((8 * chunks, LANES), f32),
                pltpu.VMEM((6 * 24, LANES), f32),
                pltpu.VMEM((2, 8, count, size, LANES), f32),
                pltpu.VMEM((2, 2, count, chunks, LANES), f32),
                pltpu.VMEM((count, size, LANES), f32),
                pltpu.SemaphoreType.DMA((2,)),
                pltpu.SemaphoreType.DMA((8,)),
                pltpu.SemaphoreType.DMA((2, groups)),
                pltpu.SemaphoreType.DMA((2, groups)),
                pltpu.SemaphoreType.DMA((2,)),
                pltpu.SemaphoreType.DMA((2,)),
                pltpu.SemaphoreType.DMA((1 + groups,)),
                pltpu.SemaphoreType.DMA((2,)),
                pltpu.SemaphoreType.DMA((11,)),
                pltpu.SemaphoreType.DMA((12,)),
                pltpu.SemaphoreType.REGULAR,
                pltpu.SemaphoreType.REGULAR,
            ],
            compiler_params=pltpu.CompilerParams(
                collective_id=0, has_side_effects=True, vmem_limit_bytes=32 * 1024 * 1024
            ),
        )(
            *map(keep, (lines(forward), lines(adjoint), log_sigma, charge, log_tau, exponent, active)),
            source_group,
            *map(keep, (group_weight, frequency_index, prior_weight)),
        )
        return result.reshape(4, 2, LANES)

    placed = (
        P("src", "freq", None, "space", None),
        P("src", "freq", None, "space", None),
        P("src"),
        P(),
        P(),
        P("space", ("src", "freq")),
        P("space", ("src", "freq")),
        P("space", ("src", "freq")),
        P("space", ("src", "freq")),
        P("space", ("src", "freq")),
        P(),
    )
    return jax.shard_map(
        local,
        mesh=mesh,
        in_specs=placed,
        out_specs=P(None, "space", ("src", "freq")),
        check_vma=False,
    )
```
